512 devices in a mesh: ctx: 64 (over z_lo, x, core), head: 8 (over y, z_hi).
Axes of the slice: x: 4, y: 4, z: 16 (z_hi: 2, z_lo: 8; z = z_hi * 8 + z_lo), core: 2. Of those that a mesh axis runs over, the one named last changes fastest.
Arguments:
- queries: bfloat16 [32768, 4096], P('ctx', 'head'), may hold values from -6 to 6
- key_vectors: bfloat16 [32768, 4096], P('ctx', 'head'), may hold values from -6 to 6
- values: bfloat16 [32768, 4096], P('ctx', 'head'), may hold values from -30 to 30
- norm_gain: float32 [4096], P('head'), may hold values from 0.1 to 1.9
- cotangent: bfloat16 [32768, 4096], P('ctx', 'head'), may hold values from -8 to 8
Outputs:
- normed_out: bfloat16 [32768, 4096], P('ctx', 'head')
- query_grad: bfloat16 [32768, 4096], P('ctx', 'head')
- key_grad: bfloat16 [32768, 4096], P('ctx', 'head')
- value_grad: bfloat16 [32768, 4096], P('ctx', 'head')
The draws below stay inside these ranges and needn't reach their ends.
All inputs are finite; a program needn't handle non-finite values.
Results may differ from the reference program's by a relative error of at most 0.015.
Values may be sent and summed in bfloat16 or wider, within the bound.
No kernel may reach another device: no remote copies, remote signals or barrier semaphores. Data moves between devices by JAX's collectives and lax.ppermute only.
A program may use at most 64 MiB of HBM per device.

```python
import jax
import jax.numpy as jnp
from jax import lax

HEADS = 32
DH = 128
TOK_DEV = 512
HD = 4096
TOKENS = 32768


def shared_channels(key):
    common = jax.random.normal(key, (1, HEADS * DH), jnp.float32)
    return jnp.clip(common, -2.0, 2.0)


def head_position():
    head_index = jnp.arange(HEADS * DH) // DH
    return head_index.astype(jnp.float32) / max(HEADS - 1, 1)


def draw_values(key, part):
    common = shared_channels(key)
    key = jax.random.fold_in(key, 7)
    position = head_position()
    scales = 10.0 ** (0.5 * position)
    normal_part = jnp.clip(jax.random.normal(key, (TOKENS, HEADS * DH), jnp.float32), -4.0, 4.0)
    sample_out = (normal_part + 0.8 * common) * scales
    return sample_out.astype(jnp.bfloat16)


def draw_cotangent(key, part):
    common = shared_channels(key)
    key = jax.random.fold_in(key, 11)
    position = head_position()
    scales = 10.0 ** (0.5 * position - 0.25)
    noise_part = 0.6 * jnp.clip(jax.random.normal(key, (TOKENS, HEADS * DH), jnp.float32), -4.0, 4.0)
    sample_out = noise_part + 0.8 * common * scales
    return sample_out.astype(jnp.bfloat16)


def block_levels(rng, shape, shards, smallest, high):
    def one(dim, shards_of):
        draws = jax.random.uniform(jax.random.fold_in(jax.random.fold_in(rng, 6), dim), (shards_of,), jnp.float32, smallest / len(shards), high / len(shards))
        return jnp.repeat(jnp.exp(draws), shape[dim] // shards_of).reshape((-1,) + (1,) * (len(shape) - dim - 1))

    gain = one(*shards[0])
    for cut in shards[1:]:
        gain = gain * one(*cut)
    return gain


def gaussian(stream_key, dims, deviation, reach, shards=(), kind=jnp.bfloat16):
    array = jax.random.normal(stream_key, dims, jnp.float32) * deviation
    if len(shards) > 0:
        array = block_levels(stream_key, dims, shards, -0.22, 0.18) * array
    return jnp.clip(array, min=-reach, max=reach).astype(kind)


def setup_inputs(seed: int = 0) -> dict:
    arg_keys = jax.random.split(jax.random.key(seed), 6)
    queries = gaussian(arg_keys[0], (TOKENS, HD), 1.0, 6.0, ((0, 64), (1, 8)))
    key_vectors = gaussian(arg_keys[1], (TOKENS, HD), 1.0, 6.0, ((0, 64), (1, 8)))
    values = draw_values(jax.random.fold_in(arg_keys[5], 71), 0)
    norm_gain = jnp.clip(1.0 + 0.18 * jax.random.normal(arg_keys[3], (HD,), jnp.float32), 0.1, 1.9)
    cotangent = draw_cotangent(jax.random.fold_in(arg_keys[5], 71), 0)
    return dict(queries=queries, key_vectors=key_vectors, values=values, norm_gain=norm_gain, cotangent=cotangent)


EPSILON = 1e-05

def reference(queries, key_vectors, values, norm_gain, cotangent):
    blocks = TOKENS // TOK_DEV
    full_width = HEADS * DH

    def split_blocks(tensor):
        return tensor.reshape(blocks, TOK_DEV, HEADS, DH)
    causal = jnp.arange(TOK_DEV)[:, None] >= jnp.arange(TOK_DEV)[None, :]

    def forward_step(state, inputs):
        query_tile, key_tile, value_tile = inputs
        query_float = query_tile.astype(jnp.float32)
        key_float = key_tile.astype(jnp.float32)
        value_float = value_tile.astype(jnp.float32)
        scores = jnp.einsum('thd,shd->hts', query_float, key_float)
        probs = lax.optimization_barrier(jnp.where(causal[None], scores, 0.0).astype(jnp.bfloat16))
        intra = jnp.einsum('hts,shd->thd', probs.astype(jnp.float32), value_float)
        state_low = lax.optimization_barrier(state.astype(jnp.bfloat16))
        inter = jnp.einsum('thd,hde->the', query_float, state_low.astype(jnp.float32))
        own_state = jnp.einsum('thd,the->hde', key_float, value_float)
        return (state + own_state, (intra + inter, state_low))
    start_state = jnp.zeros((HEADS, DH, DH), jnp.float32)
    carried, outputs = lax.scan(forward_step, start_state, (split_blocks(queries), split_blocks(key_vectors), split_blocks(values)))
    attended_blocks, prefixes = outputs
    attended = attended_blocks.reshape(TOKENS, full_width)
    inverse = lax.rsqrt(lax.optimization_barrier(jnp.mean(attended * attended, axis=-1, keepdims=True)) + EPSILON)
    normed_out = (norm_gain * attended * inverse).astype(jnp.bfloat16)
    scaled = cotangent.astype(jnp.float32) * norm_gain
    slope = lax.optimization_barrier(jnp.mean(scaled * attended, axis=-1, keepdims=True))
    attended_grad = lax.optimization_barrier((inverse * scaled - inverse * inverse * inverse * slope * attended).astype(jnp.bfloat16))

    def backward_step(later_state, inputs):
        query_tile, key_tile, value_tile, grad_tile, state_low = inputs
        query_float = query_tile.astype(jnp.float32)
        key_float = key_tile.astype(jnp.float32)
        value_float = value_tile.astype(jnp.float32)
        grad_float = grad_tile.astype(jnp.float32)
        scores = jnp.einsum('thd,shd->hts', query_float, key_float)
        probs = lax.optimization_barrier(jnp.where(causal[None], scores, 0.0).astype(jnp.bfloat16)).astype(jnp.float32)
        grad_scores = jnp.einsum('the,she->hts', grad_float, value_float)
        grad_probs = lax.optimization_barrier(jnp.where(causal[None], grad_scores, 0.0).astype(jnp.bfloat16)).astype(jnp.float32)
        later_low = lax.optimization_barrier(later_state.astype(jnp.bfloat16)).astype(jnp.float32)
        prefix_float = state_low.astype(jnp.float32)
        query_out = jnp.einsum('hts,shd->thd', grad_probs, key_float) + jnp.einsum('the,hde->thd', grad_float, prefix_float)
        key_out = jnp.einsum('hts,thd->shd', grad_probs, query_float) + jnp.einsum('she,hde->shd', value_float, later_low)
        value_out = jnp.einsum('hts,the->she', probs, grad_float) + jnp.einsum('shd,hde->she', key_float, later_low)
        own_grad = jnp.einsum('thd,the->hde', query_float, grad_float)
        return (later_state + own_grad, (query_out.astype(jnp.bfloat16), key_out.astype(jnp.bfloat16), value_out.astype(jnp.bfloat16)))
    leftover, gradients = lax.scan(backward_step, jnp.zeros((HEADS, DH, DH), jnp.float32), (split_blocks(queries), split_blocks(key_vectors), split_blocks(values), split_blocks(attended_grad), prefixes), reverse=True)
    query_blocks, key_blocks, value_blocks = gradients
    query_grad = query_blocks.reshape(TOKENS, full_width)
    key_grad = key_blocks.reshape(TOKENS, full_width)
    value_grad = value_blocks.reshape(TOKENS, full_width)
    return (normed_out, query_grad, key_grad, value_grad)
```

```python
import jax
import jax.numpy as jnp
from jax import lax
from jax.sharding import Mesh, PartitionSpec as P

DH = 128
EPSILON = 1e-05
PLANE = ("x", "core")
LINE = "z_lo"
CTX = ("z_lo", "x", "core")
HEAD = ("y", "z_hi")


def scan_states(state, backward):
    plane = lax.axis_size("x") * lax.axis_size("core")
    line = lax.axis_size(LINE)
    place = lax.axis_index(LINE)
    chunks = state.astype(jnp.bfloat16).reshape(plane, -1, DH)
    mine = lax.all_to_all(chunks, PLANE, 0, 0).astype(jnp.float32)
    order = range(plane - 1, -1, -1) if backward else range(plane)
    running = jnp.zeros(mine.shape[1:], jnp.float32)
    local = [None] * plane
    for member in order:
        local[member] = running
        running = running + mine[member]
    spread = jnp.broadcast_to(running.astype(jnp.bfloat16)[None], (line,) + running.shape)
    totals = lax.all_to_all(spread, LINE, 0, 0).astype(jnp.float32)
    index = jnp.arange(line)
    keep = index > place if backward else index < place
    outer = jnp.sum(jnp.where(keep[:, None, None], totals, 0.0), axis=0)
    low = jnp.stack([one + outer for one in local]).astype(jnp.bfloat16)
    return lax.all_to_all(low, PLANE, 0, 0).reshape(state.shape)


def on_device(queries, key_vectors, values, norm_gain, cotangent):
    row_count = queries.shape[0]
    channels = queries.shape[1]
    local_heads = channels // DH
    full_width = channels * lax.axis_size("y") * lax.axis_size("z_hi")
    members = lax.axis_size("y") * lax.axis_size("z_hi")

    def split_heads(tensor):
        return tensor.reshape(row_count, local_heads, DH)

    query_heads = split_heads(queries)
    key_heads = split_heads(key_vectors)
    value_heads = split_heads(values)
    causal = lax.broadcasted_iota(jnp.int32, (row_count, row_count), 0) >= lax.broadcasted_iota(
        jnp.int32, (row_count, row_count), 1
    )
    own_state = jnp.einsum(
        "thd,the->hde", key_heads, value_heads, preferred_element_type=jnp.float32
    )
    prefix_low = scan_states(own_state, False)
    scores = jnp.einsum("thd,shd->hts", query_heads, key_heads, preferred_element_type=jnp.float32)
    probs = jnp.where(causal[None], scores, 0.0).astype(jnp.bfloat16)
    intra = jnp.einsum("hts,shd->thd", probs, value_heads, preferred_element_type=jnp.float32)
    inter = jnp.einsum("thd,hde->the", query_heads, prefix_low, preferred_element_type=jnp.float32)
    attended = (intra + inter).reshape(row_count, channels)
    scaled = cotangent.astype(jnp.float32) * norm_gain
    squares = jnp.sum(attended * attended, axis=-1)
    slope_local = jnp.sum(scaled * attended, axis=-1)
    both = jnp.concatenate([squares, slope_local]).reshape(1, -1, DH)
    both = lax.all_to_all(jnp.broadcast_to(both, (members,) + both.shape[1:]), HEAD, 0, 0)
    both = jnp.sum(both, axis=0).reshape(2, row_count) / full_width
    inverse = lax.rsqrt(both[0] + EPSILON)[:, None]
    normed_out = (norm_gain * attended * inverse).astype(jnp.bfloat16)
    slope = both[1][:, None]
    attended_grad = (inverse * scaled - inverse * inverse * inverse * slope * attended).astype(
        jnp.bfloat16
    )
    grad_heads = split_heads(attended_grad)
    own_grad = jnp.einsum(
        "thd,the->hde", query_heads, grad_heads, preferred_element_type=jnp.float32
    )
    later_low = scan_states(own_grad, True)
    grad_scores = jnp.einsum(
        "the,she->hts", grad_heads, value_heads, preferred_element_type=jnp.float32
    )
    grad_probs = jnp.where(causal[None], grad_scores, 0.0).astype(jnp.bfloat16)
    query_total = jnp.einsum(
        "hts,shd->thd", grad_probs, key_heads, preferred_element_type=jnp.float32
    ) + jnp.einsum("the,hde->thd", grad_heads, prefix_low, preferred_element_type=jnp.float32)
    key_total = jnp.einsum(
        "hts,thd->shd", grad_probs, query_heads, preferred_element_type=jnp.float32
    ) + jnp.einsum("she,hde->shd", value_heads, later_low, preferred_element_type=jnp.float32)
    value_total = jnp.einsum(
        "hts,the->she", probs, grad_heads, preferred_element_type=jnp.float32
    ) + jnp.einsum("shd,hde->she", key_heads, later_low, preferred_element_type=jnp.float32)
    query_grad = query_total.reshape(row_count, channels).astype(jnp.bfloat16)
    key_grad = key_total.reshape(row_count, channels).astype(jnp.bfloat16)
    value_grad = value_total.reshape(row_count, channels).astype(jnp.bfloat16)
    return (normed_out, query_grad, key_grad, value_grad)


def solution(mesh):
    fine = Mesh(
        mesh.devices.reshape(8, 4, 2, 4, 2), ("z_lo", "x", "core", "y", "z_hi")
    )
    placed = (P(CTX, HEAD), P(CTX, HEAD), P(CTX, HEAD), P(HEAD), P(CTX, HEAD))
    return jax.shard_map(
        on_device,
        mesh=fine,
        in_specs=placed,
        out_specs=(P(CTX, HEAD),) * 4,
        check_vma=False,
    )
```

```python
import functools

import jax
import jax.numpy as jnp
from jax import lax
from jax.experimental import pallas as pl
from jax.experimental.pallas import tpu as pltpu
from jax.sharding import Mesh, PartitionSpec as P

DH = 128
EPSILON = 1e-05
PLANE = ("x", "core")
LINE = "z_lo"
CTX = ("z_lo", "x", "core")
HEAD = ("y", "z_hi")
LOW = jnp.bfloat16
WIDE = jnp.float32


def dot(left, right, left_dim, right_dim):
    return lax.dot_general(
        left, right, (((left_dim,), (right_dim,)), ((), ())), preferred_element_type=WIDE
    )


def head_columns(head):
    return slice(head * DH, (head + 1) * DH)


def state_of(low_ref, head):
    rows = low_ref.shape[1]
    per_head = DH // rows
    return low_ref[head * per_head : (head + 1) * per_head].reshape(DH, DH)


def put_state(out_ref, head, state):
    rows = out_ref.shape[1]
    per_head = DH // rows
    out_ref[head * per_head : (head + 1) * per_head] = state.astype(LOW).reshape(
        per_head, rows, DH
    )


def causal_tile(size):
    return lax.broadcasted_iota(jnp.int32, (size, size), 0) >= lax.broadcasted_iota(
        jnp.int32, (size, size), 1
    )


def own_state_kernel(left_ref, right_ref, out_ref):
    for head in range(left_ref.shape[1] // DH):
        at = head_columns(head)
        put_state(out_ref, head, dot(left_ref[:, at], right_ref[:, at], 0, 0))


def masked_tiles(left_ref, right_ref, at, out_ref, head):
    half = left_ref.shape[0] // 2
    causal = causal_tile(half)
    first = dot(left_ref[:, at], right_ref[:half, at], 1, 1)
    last = dot(left_ref[half:, at], right_ref[half:, at], 1, 1)
    out_ref[head, :half] = jnp.where(causal, first[:half], 0.0).astype(LOW)
    out_ref[head, half : 2 * half] = first[half:].astype(LOW)
    out_ref[head, 2 * half :] = jnp.where(causal, last, 0.0).astype(LOW)


def rows_product(tiles_ref, head, right_ref, at):
    half = tiles_ref.shape[2]
    both = dot(tiles_ref[head, : 2 * half], right_ref[:half, at], 1, 0)
    last = dot(tiles_ref[head, 2 * half :], right_ref[half:, at], 1, 0)
    return both[:half], both[half:] + last


def columns_product(tiles_ref, head, right_ref, at):
    half = tiles_ref.shape[2]
    first = dot(tiles_ref[head, : 2 * half], right_ref[:, at], 0, 0)
    last = dot(tiles_ref[head, 2 * half :], right_ref[half:, at], 0, 0)
    return first, last


def intra_kernel(query_ref, key_ref, value_ref, tiles_ref, intra_ref):
    half = query_ref.shape[0] // 2
    for head in range(query_ref.shape[1] // DH):
        at = head_columns(head)
        masked_tiles(query_ref, key_ref, at, tiles_ref, head)
        top, bottom = rows_product(tiles_ref, head, value_ref, at)
        intra_ref[:half, at] = top
        intra_ref[half:, at] = bottom


def totals_kernel(mine_ref, out_ref):
    total = mine_ref[0].astype(WIDE)
    for member in range(1, mine_ref.shape[0]):
        total = total + mine_ref[member].astype(WIDE)
    out_ref[...] = jnp.broadcast_to(total.astype(LOW)[None], out_ref.shape)


def chunks_kernel(backward, place_ref, mine_ref, totals_ref, out_ref):
    place = place_ref[0]
    running = jnp.zeros(mine_ref.shape[1:], WIDE)
    for plane in range(totals_ref.shape[0]):
        keep = plane > place if backward else plane < place
        running = running + jnp.where(keep, totals_ref[plane].astype(WIDE), 0.0)
    members = mine_ref.shape[0]
    for member in range(members - 1, -1, -1) if backward else range(members):
        out_ref[member] = running.astype(LOW)
        running = running + mine_ref[member].astype(WIDE)


def attend_kernel(query_ref, low_ref, intra_ref, cotangent_ref, gain_ref, attended_ref, sums_ref):
    rows, channels = query_ref.shape
    squares = jnp.zeros((rows, DH), WIDE)
    slopes = jnp.zeros((rows, DH), WIDE)
    for head in range(channels // DH):
        at = head_columns(head)
        attended = intra_ref[:, at] + dot(query_ref[:, at], state_of(low_ref, head), 1, 0)
        attended_ref[:, at] = attended
        squares = squares + attended * attended
        slopes = slopes + cotangent_ref[:, at].astype(WIDE) * gain_ref[:, at] * attended
    parts = []
    for sums in (squares, slopes):
        for block in range(rows // DH):
            turned = jnp.transpose(sums[block * DH : (block + 1) * DH])
            parts.append(jnp.sum(turned, axis=0, keepdims=True))
    packed = jnp.concatenate(parts, axis=0)
    sums_ref[...] = jnp.broadcast_to(packed[None], sums_ref.shape)


def grad_kernel(
    full_width, sums_ref, attended_ref, cotangent_ref, gain_ref, query_ref,
    grad_ref, own_ref, inverse_ref,
):
    rows, channels = query_ref.shape
    blocks = rows // DH
    total = sums_ref[0]
    for member in range(1, sums_ref.shape[0]):
        total = total + sums_ref[member]
    mean = total * (1.0 / full_width)
    inverse = lax.rsqrt(mean[:blocks] + EPSILON)
    factor = inverse * inverse * inverse * mean[blocks:]
    for block in range(blocks):
        at_rows = slice(block * DH, (block + 1) * DH)
        wide = jnp.transpose(jnp.broadcast_to(inverse[block : block + 1], (DH, DH)))
        second = jnp.transpose(jnp.broadcast_to(factor[block : block + 1], (DH, DH)))
        inverse_ref[at_rows] = wide
        for head in range(channels // DH):
            at = head_columns(head)
            scaled = cotangent_ref[at_rows, at].astype(WIDE) * gain_ref[:, at]
            grad_ref[at_rows, at] = (
                wide * scaled - second * attended_ref[at_rows, at]
            ).astype(LOW)
    for head in range(channels // DH):
        at = head_columns(head)
        put_state(own_ref, head, dot(query_ref[:, at], grad_ref[:, at], 0, 0))


def query_grad_kernel(
    grad_ref, key_ref, value_ref, low_ref, attended_ref, inverse_ref, gain_ref,
    grad_tiles_ref, query_grad_ref, normed_ref,
):
    half = grad_ref.shape[0] // 2
    inverse = inverse_ref[...]
    for head in range(grad_ref.shape[1] // DH):
        at = head_columns(head)
        masked_tiles(grad_ref, value_ref, at, grad_tiles_ref, head)
        inter = dot(grad_ref[:, at], state_of(low_ref, head), 1, 1)
        top, bottom = rows_product(grad_tiles_ref, head, key_ref, at)
        query_grad_ref[:half, at] = (top + inter[:half]).astype(LOW)
        query_grad_ref[half:, at] = (bottom + inter[half:]).astype(LOW)
        normed_ref[:, at] = (gain_ref[:, at] * attended_ref[:, at] * inverse).astype(LOW)


def partial_kernel(
    grad_ref, query_ref, tiles_ref, grad_tiles_ref, key_part_ref, value_part_ref
):
    half = grad_ref.shape[0] // 2
    for head in range(grad_ref.shape[1] // DH):
        at = head_columns(head)
        first, last = columns_product(grad_tiles_ref, head, query_ref, at)
        key_part_ref[:half, at] = first
        key_part_ref[half:, at] = last
        first, last = columns_product(tiles_ref, head, grad_ref, at)
        value_part_ref[:half, at] = first
        value_part_ref[half:, at] = last


def final_kernel(
    key_ref, value_ref, later_ref, key_part_ref, value_part_ref, key_grad_ref, value_grad_ref
):
    for head in range(key_ref.shape[1] // DH):
        at = head_columns(head)
        later = state_of(later_ref, head)
        key_grad_ref[:, at] = (
            key_part_ref[:, at] + dot(value_ref[:, at], later, 1, 1)
        ).astype(LOW)
        value_grad_ref[:, at] = (
            value_part_ref[:, at] + dot(key_ref[:, at], later, 1, 0)
        ).astype(LOW)


IN_VMEM = pl.BlockSpec(memory_space=pltpu.VMEM)
IN_SMEM = pl.BlockSpec(memory_space=pltpu.SMEM)


def call(kernel, shapes, *operands, flops=0, scalars=0, mib=8):
    outs = tuple(jax.ShapeDtypeStruct(shape, kind) for shape, kind in shapes)
    moved = sum(a.size * a.dtype.itemsize for a in operands) + sum(
        o.size * o.dtype.itemsize for o in outs
    )
    return pl.pallas_call(
        kernel,
        out_shape=outs,
        in_specs=[IN_SMEM] * scalars + [IN_VMEM] * (len(operands) - scalars),
        out_specs=tuple(IN_VMEM for _ in outs),
        compiler_params=pltpu.CompilerParams(vmem_limit_bytes=mib * 2**20),
        cost_estimate=pl.CostEstimate(flops=flops, bytes_accessed=moved, transcendentals=0),
    )(*operands)


def scan_states(chunks, place, backward):
    shape = (chunks.shape, LOW)
    line = lax.axis_size(LINE)
    mine = lax.all_to_all(chunks, PLANE, 0, 0)
    (spread,) = call(totals_kernel, [((line,) + mine.shape[1:], LOW)], mine)
    totals = lax.all_to_all(spread, LINE, 0, 0)
    (low,) = call(
        functools.partial(chunks_kernel, backward), [shape], place, mine, totals, scalars=1
    )
    return lax.all_to_all(low, PLANE, 0, 0)


def on_device(queries, key_vectors, values, norm_gain, cotangent):
    rows, channels = queries.shape
    heads = channels // DH
    half = rows // 2
    members = lax.axis_size("y") * lax.axis_size("z_hi")
    plane = lax.axis_size("x") * lax.axis_size("core")
    full_width = channels * members
    place = lax.axis_index(LINE).astype(jnp.int32).reshape(1)
    gain = norm_gain.reshape(1, channels)
    unit = 2 * rows * DH * DH * heads
    chunks = ((plane, channels // plane, DH), LOW)
    tiles = ((heads, 3 * half, half), LOW)
    whole = ((rows, channels), WIDE)
    result = ((rows, channels), LOW)

    (own,) = call(own_state_kernel, [chunks], key_vectors, values, flops=unit)
    prefix_low = scan_states(own, place, False)
    probs, intra = call(
        intra_kernel, [tiles, whole], queries, key_vectors, values, flops=6 * unit
    )
    attended, sums = call(
        attend_kernel,
        [whole, ((members, 2 * rows // DH, DH), WIDE)],
        queries, prefix_low, intra, cotangent, gain, flops=unit,
    )
    sums = lax.all_to_all(sums, HEAD, 0, 0)
    grad, own_grad, inverse = call(
        functools.partial(grad_kernel, full_width),
        [result, chunks, ((rows, DH), WIDE)],
        sums, attended, cotangent, gain, queries, flops=unit,
    )
    later_low = scan_states(own_grad, place, True)
    grad_probs, query_grad, normed_out = call(
        query_grad_kernel,
        [tiles, result, result],
        grad, key_vectors, values, prefix_low, attended, inverse, gain, flops=7 * unit,
    )
    key_part, value_part = call(
        partial_kernel, [whole, whole], grad, queries, probs, grad_probs, flops=6 * unit
    )
    key_grad, value_grad = call(
        final_kernel,
        [result, result],
        key_vectors, values, later_low, key_part, value_part, flops=2 * unit,
    )
    return (normed_out, query_grad, key_grad, value_grad)


def solution(mesh):
    fine = Mesh(
        mesh.devices.reshape(8, 4, 2, 4, 2), ("z_lo", "x", "core", "y", "z_hi")
    )
    placed = (P(CTX, HEAD), P(CTX, HEAD), P(CTX, HEAD), P(HEAD), P(CTX, HEAD))
    return jax.shard_map(
        on_device,
        mesh=fine,
        in_specs=placed,
        out_specs=(P(CTX, HEAD),) * 4,
        check_vma=False,
    )
```

```python
import functools

import jax
import jax.numpy as jnp
from jax import lax
from jax.experimental import pallas as pl
from jax.experimental.pallas import tpu as pltpu
from jax.sharding import Mesh, PartitionSpec as P

DH = 128
EPSILON = 1e-05
PLANE = ("x", "core")
LINE = "z_lo"
CTX = ("z_lo", "x", "core")
HEAD = ("y", "z_hi")
LOW = jnp.bfloat16
WIDE = jnp.float32


def dot(left, right, left_dim, right_dim):
    return lax.dot_general(
        left, right, (((left_dim,), (right_dim,)), ((), ())), preferred_element_type=WIDE
    )


def head_columns(head):
    return slice(head * DH, (head + 1) * DH)


def state_of(low_ref, head):
    rows = low_ref.shape[1]
    per_head = DH // rows
    return low_ref[head * per_head : (head + 1) * per_head].reshape(DH, DH)


def put_state(out_ref, head, state):
    rows = out_ref.shape[1]
    per_head = DH // rows
    out_ref[head * per_head : (head + 1) * per_head] = state.astype(LOW).reshape(
        per_head, rows, DH
    )


def causal_tile(size):
    return lax.broadcasted_iota(jnp.int32, (size, size), 0) >= lax.broadcasted_iota(
        jnp.int32, (size, size), 1
    )


def own_state_kernel(place_ref, left_hbm, right_hbm, out_ref, left_ref, right_ref, total_ref, sems):
    rows, channels = left_ref.shape
    copies = []
    for block in range(rows // DH):
        at = pl.ds(block * DH, DH)
        for side, (source, target) in enumerate(((left_hbm, left_ref), (right_hbm, right_ref))):
            copies.append(pltpu.make_async_copy(source.at[at], target.at[at], sems.at[side, block]))
            copies[-1].start()
    half = rows // 2
    for part in range(2):
        for copy in copies[part * len(copies) // 2 : (part + 1) * len(copies) // 2]:
            copy.wait()
        at_rows = slice(part * half, (part + 1) * half)
        for head in range(channels // DH):
            at = head_columns(head)
            state = dot(left_ref[at_rows, at], right_ref[at_rows, at], 0, 0)
            if part == 0:
                total_ref[head] = state
            else:
                put_state(out_ref, head, total_ref[head] + state)


def masked_tiles(left_ref, right_ref, at, out_ref, head):
    half = left_ref.shape[0] // 2
    causal = causal_tile(half)
    first = dot(left_ref[:, at], right_ref[:half, at], 1, 1)
    last = dot(left_ref[half:, at], right_ref[half:, at], 1, 1)
    out_ref[head, :half] = jnp.where(causal, first[:half], 0.0).astype(LOW)
    out_ref[head, half : 2 * half] = first[half:].astype(LOW)
    out_ref[head, 2 * half :] = jnp.where(causal, last, 0.0).astype(LOW)


def rows_product(tiles_ref, head, right_ref, at):
    half = tiles_ref.shape[2]
    both = dot(tiles_ref[head, : 2 * half], right_ref[:half, at], 1, 0)
    last = dot(tiles_ref[head, 2 * half :], right_ref[half:, at], 1, 0)
    return both[:half], both[half:] + last


def columns_product(tiles_ref, head, right_ref, at):
    half = tiles_ref.shape[2]
    first = dot(tiles_ref[head, : 2 * half], right_ref[:, at], 0, 0)
    last = dot(tiles_ref[head, 2 * half :], right_ref[half:, at], 0, 0)
    return first, last


def intra_kernel(query_ref, key_ref, value_ref, after_ref, intra_ref, tiles_ref):
    half = query_ref.shape[0] // 2
    for head in range(query_ref.shape[1] // DH):
        at = head_columns(head)
        masked_tiles(query_ref, key_ref, at, tiles_ref, head)
        top, bottom = rows_product(tiles_ref, head, value_ref, at)
        intra_ref[:half, at] = top
        intra_ref[half:, at] = bottom


def totals_kernel(mine_ref, out_ref):
    total = mine_ref[0].astype(WIDE)
    for member in range(1, mine_ref.shape[0]):
        total = total + mine_ref[member].astype(WIDE)
    out_ref[...] = jnp.broadcast_to(total.astype(LOW)[None], out_ref.shape)


def chunks_kernel(backward, place_ref, mine_ref, totals_ref, *rest):
    out_ref = rest[-1]
    place = place_ref[0]
    running = jnp.zeros(mine_ref.shape[1:], WIDE)
    for plane in range(totals_ref.shape[0]):
        keep = plane > place if backward else plane < place
        running = running + jnp.where(keep, totals_ref[plane].astype(WIDE), 0.0)
    members = mine_ref.shape[0]
    for member in range(members - 1, -1, -1) if backward else range(members):
        out_ref[member] = running.astype(LOW)
        running = running + mine_ref[member].astype(WIDE)


def attend_kernel(query_ref, low_ref, intra_ref, cotangent_ref, gain_ref, attended_ref, sums_ref):
    rows, channels = query_ref.shape
    squares = jnp.zeros((rows, DH), WIDE)
    slopes = jnp.zeros((rows, DH), WIDE)
    for head in range(channels // DH):
        at = head_columns(head)
        attended = intra_ref[:, at] + dot(query_ref[:, at], state_of(low_ref, head), 1, 0)
        attended_ref[:, at] = attended
        squares = squares + attended * attended
        slopes = slopes + cotangent_ref[:, at].astype(WIDE) * gain_ref[:, at] * attended
    parts = []
    for sums in (squares, slopes):
        for block in range(rows // DH):
            turned = jnp.transpose(sums[block * DH : (block + 1) * DH])
            parts.append(jnp.sum(turned, axis=0, keepdims=True))
    packed = jnp.concatenate(parts, axis=0)
    sums_ref[...] = jnp.broadcast_to(packed[None], sums_ref.shape)


def grad_kernel(
    full_width, sums_ref, attended_ref, cotangent_ref, gain_ref, query_ref,
    grad_ref, own_ref, inverse_ref,
):
    rows, channels = query_ref.shape
    blocks = rows // DH
    total = sums_ref[0]
    for member in range(1, sums_ref.shape[0]):
        total = total + sums_ref[member]
    mean = total * (1.0 / full_width)
    inverse = lax.rsqrt(mean[:blocks] + EPSILON)
    factor = inverse * inverse * inverse * mean[blocks:]
    for block in range(blocks):
        at_rows = slice(block * DH, (block + 1) * DH)
        wide = jnp.transpose(jnp.broadcast_to(inverse[block : block + 1], (DH, DH)))
        second = jnp.transpose(jnp.broadcast_to(factor[block : block + 1], (DH, DH)))
        inverse_ref[at_rows] = wide
        for head in range(channels // DH):
            at = head_columns(head)
            scaled = cotangent_ref[at_rows, at].astype(WIDE) * gain_ref[:, at]
            grad_ref[at_rows, at] = (
                wide * scaled - second * attended_ref[at_rows, at]
            ).astype(LOW)
    for head in range(channels // DH):
        at = head_columns(head)
        put_state(own_ref, head, dot(query_ref[:, at], grad_ref[:, at], 0, 0))


def products_kernel(
    grad_ref, query_ref, key_ref, value_ref, low_ref, attended_ref, inverse_ref, gain_ref, after_ref,
    query_grad_ref, normed_ref, key_part_ref, value_part_ref, tiles_ref, grad_tiles_ref,
):
    half = grad_ref.shape[0] // 2
    inverse = inverse_ref[...]
    for head in range(grad_ref.shape[1] // DH):
        at = head_columns(head)
        masked_tiles(query_ref, key_ref, at, tiles_ref, head)
        masked_tiles(grad_ref, value_ref, at, grad_tiles_ref, head)
        inter = dot(grad_ref[:, at], state_of(low_ref, head), 1, 1)
        top, bottom = rows_product(grad_tiles_ref, head, key_ref, at)
        query_grad_ref[:half, at] = (top + inter[:half]).astype(LOW)
        query_grad_ref[half:, at] = (bottom + inter[half:]).astype(LOW)
        normed_ref[:, at] = (gain_ref[:, at] * attended_ref[:, at] * inverse).astype(LOW)
        first, last = columns_product(grad_tiles_ref, head, query_ref, at)
        key_part_ref[:half, at] = first
        key_part_ref[half:, at] = last
        first, last = columns_product(tiles_ref, head, grad_ref, at)
        value_part_ref[:half, at] = first
        value_part_ref[half:, at] = last


def final_kernel(
    key_ref, value_ref, later_ref, key_part_ref, value_part_ref, key_grad_hbm, value_grad_hbm,
    key_grad_ref, value_grad_ref, sems,
):
    rows, channels = key_ref.shape
    copies = []
    for block in range(rows // DH):
        at_rows = slice(block * DH, (block + 1) * DH)
        for head in range(channels // DH):
            at = head_columns(head)
            later = state_of(later_ref, head)
            key_grad_ref[at_rows, at] = (
                key_part_ref[at_rows, at] + dot(value_ref[at_rows, at], later, 1, 1)
            ).astype(LOW)
            value_grad_ref[at_rows, at] = (
                value_part_ref[at_rows, at] + dot(key_ref[at_rows, at], later, 1, 0)
            ).astype(LOW)
        span = pl.ds(block * DH, DH)
        for side, (source, target) in enumerate(
            ((key_grad_ref, key_grad_hbm), (value_grad_ref, value_grad_hbm))
        ):
            copies.append(pltpu.make_async_copy(source.at[span], target.at[span], sems.at[side, block]))
            copies[-1].start()
    for copy in copies:
        copy.wait()


IN_VMEM = pl.BlockSpec(memory_space=pltpu.VMEM)
IN_SMEM = pl.BlockSpec(memory_space=pltpu.SMEM)
ANYWHERE = pl.BlockSpec(memory_space=pl.ANY)
IN_HBM = pl.BlockSpec(memory_space=pltpu.HBM)


def call(kernel, shapes, *operands, flops=0, places="", out_places="", scratch=(), mib=8):
    kinds = {"v": IN_VMEM, "s": IN_SMEM, "a": ANYWHERE, "h": IN_HBM}
    outs = tuple(jax.ShapeDtypeStruct(shape, kind) for shape, kind in shapes)
    moved = sum(a.size * a.dtype.itemsize for a in operands) + sum(
        o.size * o.dtype.itemsize for o in outs
    )
    return pl.pallas_call(
        kernel,
        out_shape=outs,
        in_specs=[kinds[k] for k in places or "v" * len(operands)],
        out_specs=tuple(kinds[k] for k in out_places or "v" * len(outs)),
        scratch_shapes=scratch,
        compiler_params=pltpu.CompilerParams(vmem_limit_bytes=int(mib * 2**20)),
        cost_estimate=pl.CostEstimate(flops=flops, bytes_accessed=moved, transcendentals=0),
    )(*operands)


def scan_states(chunks, place, backward, beside=None):
    shape = (chunks.shape, LOW)
    line = lax.axis_size(LINE)
    mine = lax.all_to_all(chunks, PLANE, 0, 0)
    (spread,) = call(totals_kernel, [((line,) + mine.shape[1:], LOW)], mine)
    totals = lax.all_to_all(spread, LINE, 0, 0)
    extra = () if beside is None else tuple(beside(spread))
    order = extra[-1:]
    (low,) = call(
        functools.partial(chunks_kernel, backward), [shape], place, mine, totals, *order,
        places="svv" + "a" * len(order),
    )
    return low, extra


def on_device(queries, key_vectors, values, norm_gain, cotangent):
    rows, channels = queries.shape
    heads = channels // DH
    half = rows // 2
    members = lax.axis_size("y") * lax.axis_size("z_hi")
    plane = lax.axis_size("x") * lax.axis_size("core")
    full_width = channels * members
    place = lax.axis_index(LINE).astype(jnp.int32).reshape(1)
    gain = norm_gain.reshape(1, channels)
    unit = 2 * rows * DH * DH * heads
    chunks = ((plane, channels // plane, DH), LOW)
    whole = ((rows, channels), WIDE)
    result = ((rows, channels), LOW)
    buffer = pltpu.VMEM(*result)
    tiles = pltpu.VMEM((heads, 3 * half, half), LOW)
    sems = pltpu.SemaphoreType.DMA((2, rows // DH))

    (own,) = call(
        own_state_kernel, [chunks], place, key_vectors, values, flops=unit, places="shh",
        scratch=[buffer, buffer, pltpu.VMEM((heads, DH, DH), WIDE), sems], mib=53.6,
    )
    low, _ = scan_states(own, place, False)
    prefix_low = lax.all_to_all(low, PLANE, 0, 0)
    (intra,) = call(
        intra_kernel, [whole], queries, key_vectors, values, low, flops=6 * unit,
        places="vvva", scratch=[tiles],
    )
    attended, sums = call(
        attend_kernel,
        [whole, ((members, 2 * rows // DH, DH), WIDE)],
        queries, prefix_low, intra, cotangent, gain, flops=unit,
    )
    sums = lax.all_to_all(sums, HEAD, 0, 0)
    grad, own_grad, inverse = call(
        functools.partial(grad_kernel, full_width),
        [result, chunks, ((rows, DH), WIDE)],
        sums, attended, cotangent, gain, queries, flops=unit,
    )

    def products(after):
        return call(
            products_kernel,
            [result, result, whole, whole],
            grad, queries, key_vectors, values, prefix_low, attended, inverse, gain, after,
            flops=16 * unit, places="vvvvvvvva", scratch=[tiles, tiles], mib=10,
        )

    low, extra = scan_states(own_grad, place, True, products)
    query_grad, normed_out, key_part, value_part = extra
    later_low = lax.all_to_all(low, PLANE, 0, 0)
    key_grad, value_grad = call(
        final_kernel,
        [result, result],
        key_vectors, values, later_low, key_part, value_part, flops=2 * unit,
        out_places="hh", scratch=[buffer, buffer, sems],
    )
    return (normed_out, query_grad, key_grad, value_grad)


def solution(mesh):
    fine = Mesh(
        mesh.devices.reshape(8, 4, 2, 4, 2), ("z_lo", "x", "core", "y", "z_hi")
    )
    placed = (P(CTX, HEAD), P(CTX, HEAD), P(CTX, HEAD), P(HEAD), P(CTX, HEAD))
    return jax.shard_map(
        on_device,
        mesh=fine,
        in_specs=placed,
        out_specs=(P(CTX, HEAD),) * 4,
        check_vma=False,
    )
```

```python
import functools

import jax
import jax.numpy as jnp
from jax import lax
from jax.experimental import pallas as pl
from jax.experimental.pallas import tpu as pltpu
from jax.sharding import Mesh, PartitionSpec as P

DH = 128
EPSILON = 1e-05
PLANE = ("x", "core")
LINE = "z_lo"
CTX = ("z_lo", "x", "core")
HEAD = ("y", "z_hi")
LINE_ORDER = [7, 6, 5, 4, 3, 2, 1, 0]
PLANE_ORDER = [4, 5, 6, 7, 0, 1, 2, 3]
HEAD_ORDER = [5, 7, 1, 3, 4, 6, 0, 2]
LOW = jnp.bfloat16
WIDE = jnp.float32


def dot(left, right, left_dim, right_dim):
    return lax.dot_general(
        left, right, (((left_dim,), (right_dim,)), ((), ())), preferred_element_type=WIDE
    )


def head_columns(head):
    return slice(head * DH, (head + 1) * DH)


def state_of(low_ref, head):
    rows = low_ref.shape[1]
    per_head = DH // rows
    return low_ref[head * per_head : (head + 1) * per_head].reshape(DH, DH)


def put_state(out_ref, head, state):
    rows = out_ref.shape[1]
    per_head = DH // rows
    out_ref[head * per_head : (head + 1) * per_head] = state.astype(LOW).reshape(
        per_head, rows, DH
    )


def causal_tile(size):
    return lax.broadcasted_iota(jnp.int32, (size, size), 0) >= lax.broadcasted_iota(
        jnp.int32, (size, size), 1
    )


def own_state_kernel(place_ref, left_hbm, right_hbm, out_ref, left_ref, right_ref, total_ref, sems):
    rows, channels = left_ref.shape
    copies = []
    for block in range(rows // DH):
        at = pl.ds(block * DH, DH)
        for side, (source, target) in enumerate(((left_hbm, left_ref), (right_hbm, right_ref))):
            copies.append(pltpu.make_async_copy(source.at[at], target.at[at], sems.at[side, block]))
            copies[-1].start()
    half = rows // 2
    for part in range(2):
        for copy in copies[part * len(copies) // 2 : (part + 1) * len(copies) // 2]:
            copy.wait()
        at_rows = slice(part * half, (part + 1) * half)
        for head in range(channels // DH):
            at = head_columns(head)
            state = dot(left_ref[at_rows, at], right_ref[at_rows, at], 0, 0)
            if part == 0:
                total_ref[head] = state
            else:
                put_state(out_ref, head, total_ref[head] + state)


def masked_tiles(left_ref, right_ref, at, out_ref, head):
    half = left_ref.shape[0] // 2
    causal = causal_tile(half)
    first = dot(left_ref[:, at], right_ref[:half, at], 1, 1)
    last = dot(left_ref[half:, at], right_ref[half:, at], 1, 1)
    out_ref[head, :half] = jnp.where(causal, first[:half], 0.0).astype(LOW)
    out_ref[head, half : 2 * half] = first[half:].astype(LOW)
    out_ref[head, 2 * half :] = jnp.where(causal, last, 0.0).astype(LOW)


def rows_product(tiles_ref, head, right_ref, at):
    half = tiles_ref.shape[2]
    both = dot(tiles_ref[head, : 2 * half], right_ref[:half, at], 1, 0)
    last = dot(tiles_ref[head, 2 * half :], right_ref[half:, at], 1, 0)
    return both[:half], both[half:] + last


def columns_product(tiles_ref, head, right_ref, at):
    half = tiles_ref.shape[2]
    first = dot(tiles_ref[head, : 2 * half], right_ref[:, at], 0, 0)
    last = dot(tiles_ref[head, 2 * half :], right_ref[half:, at], 0, 0)
    return first, last


def intra_kernel(query_ref, key_ref, value_ref, after_ref, intra_ref, tiles_ref):
    half = query_ref.shape[0] // 2
    for head in range(query_ref.shape[1] // DH):
        at = head_columns(head)
        masked_tiles(query_ref, key_ref, at, tiles_ref, head)
        top, bottom = rows_product(tiles_ref, head, value_ref, at)
        intra_ref[:half, at] = top
        intra_ref[half:, at] = bottom


def totals_kernel(mine_ref, out_ref):
    total = mine_ref[0].astype(WIDE)
    for member in range(1, mine_ref.shape[0]):
        total = total + mine_ref[member].astype(WIDE)
    out_ref[...] = jnp.broadcast_to(total.astype(LOW)[None], out_ref.shape)


def chunks_kernel(backward, place_ref, mine_ref, totals_ref, *rest):
    out_ref = rest[-1]
    place = place_ref[0]
    running = jnp.zeros(mine_ref.shape[1:], WIDE)
    for slot, plane in enumerate(LINE_ORDER):
        keep = plane > place if backward else plane < place
        running = running + jnp.where(keep, totals_ref[slot].astype(WIDE), 0.0)
    members = mine_ref.shape[0]
    for member in range(members - 1, -1, -1) if backward else range(members):
        slot = PLANE_ORDER.index(member)
        out_ref[slot] = running.astype(LOW)
        running = running + mine_ref[slot].astype(WIDE)


def attend_kernel(query_ref, low_ref, intra_ref, cotangent_ref, gain_ref, attended_ref, sums_ref):
    rows, channels = query_ref.shape
    squares = jnp.zeros((rows, DH), WIDE)
    slopes = jnp.zeros((rows, DH), WIDE)
    for head in range(channels // DH):
        at = head_columns(head)
        attended = intra_ref[:, at] + dot(query_ref[:, at], state_of(low_ref, head), 1, 0)
        attended_ref[:, at] = attended
        squares = squares + attended * attended
        slopes = slopes + cotangent_ref[:, at].astype(WIDE) * gain_ref[:, at] * attended
    parts = []
    for sums in (squares, slopes):
        for block in range(rows // DH):
            turned = jnp.transpose(sums[block * DH : (block + 1) * DH])
            parts.append(jnp.sum(turned, axis=0, keepdims=True))
    packed = jnp.concatenate(parts, axis=0)
    sums_ref[...] = jnp.broadcast_to(packed[None], sums_ref.shape)


def grad_kernel(
    full_width, sums_ref, attended_ref, cotangent_ref, gain_ref, query_ref,
    grad_ref, own_ref, inverse_ref,
):
    rows, channels = query_ref.shape
    blocks = rows // DH
    total = sums_ref[0]
    for member in range(1, sums_ref.shape[0]):
        total = total + sums_ref[member]
    mean = total * (1.0 / full_width)
    inverse = lax.rsqrt(mean[:blocks] + EPSILON)
    factor = inverse * inverse * inverse * mean[blocks:]
    for block in range(blocks):
        at_rows = slice(block * DH, (block + 1) * DH)
        wide = jnp.transpose(jnp.broadcast_to(inverse[block : block + 1], (DH, DH)))
        second = jnp.transpose(jnp.broadcast_to(factor[block : block + 1], (DH, DH)))
        inverse_ref[at_rows] = wide
        for head in range(channels // DH):
            at = head_columns(head)
            scaled = cotangent_ref[at_rows, at].astype(WIDE) * gain_ref[:, at]
            grad_ref[at_rows, at] = (
                wide * scaled - second * attended_ref[at_rows, at]
            ).astype(LOW)
    for head in range(channels // DH):
        at = head_columns(head)
        put_state(own_ref, head, dot(query_ref[:, at], grad_ref[:, at], 0, 0))


def products_kernel(
    grad_ref, query_ref, key_ref, value_ref, low_ref, attended_ref, inverse_ref, gain_ref, after_ref,
    query_grad_ref, normed_ref, key_part_ref, value_part_ref, tiles_ref, grad_tiles_ref,
):
    half = grad_ref.shape[0] // 2
    inverse = inverse_ref[...]
    for head in range(grad_ref.shape[1] // DH):
        at = head_columns(head)
        masked_tiles(query_ref, key_ref, at, tiles_ref, head)
        masked_tiles(grad_ref, value_ref, at, grad_tiles_ref, head)
        inter = dot(grad_ref[:, at], state_of(low_ref, head), 1, 1)
        top, bottom = rows_product(grad_tiles_ref, head, key_ref, at)
        query_grad_ref[:half, at] = (top + inter[:half]).astype(LOW)
        query_grad_ref[half:, at] = (bottom + inter[half:]).astype(LOW)
        normed_ref[:, at] = (gain_ref[:, at] * attended_ref[:, at] * inverse).astype(LOW)
        first, last = columns_product(grad_tiles_ref, head, query_ref, at)
        key_part_ref[:half, at] = first
        key_part_ref[half:, at] = last
        first, last = columns_product(tiles_ref, head, grad_ref, at)
        value_part_ref[:half, at] = first
        value_part_ref[half:, at] = last


def final_kernel(
    key_ref, value_ref, later_ref, key_part_ref, value_part_ref, key_grad_hbm, value_grad_hbm,
    key_grad_ref, value_grad_ref, sems,
):
    rows, channels = key_ref.shape
    copies = []
    for block in range(rows // DH):
        at_rows = slice(block * DH, (block + 1) * DH)
        for head in range(channels // DH):
            at = head_columns(head)
            later = state_of(later_ref, head)
            key_grad_ref[at_rows, at] = (
                key_part_ref[at_rows, at] + dot(value_ref[at_rows, at], later, 1, 1)
            ).astype(LOW)
            value_grad_ref[at_rows, at] = (
                value_part_ref[at_rows, at] + dot(key_ref[at_rows, at], later, 1, 0)
            ).astype(LOW)
        span = pl.ds(block * DH, DH)
        for side, (source, target) in enumerate(
            ((key_grad_ref, key_grad_hbm), (value_grad_ref, value_grad_hbm))
        ):
            copies.append(pltpu.make_async_copy(source.at[span], target.at[span], sems.at[side, block]))
            copies[-1].start()
    for copy in copies:
        copy.wait()


IN_VMEM = pl.BlockSpec(memory_space=pltpu.VMEM)
IN_SMEM = pl.BlockSpec(memory_space=pltpu.SMEM)
ANYWHERE = pl.BlockSpec(memory_space=pl.ANY)
IN_HBM = pl.BlockSpec(memory_space=pltpu.HBM)


def call(kernel, shapes, *operands, flops=0, places="", out_places="", scratch=(), mib=8):
    kinds = {"v": IN_VMEM, "s": IN_SMEM, "a": ANYWHERE, "h": IN_HBM}
    outs = tuple(jax.ShapeDtypeStruct(shape, kind) for shape, kind in shapes)
    moved = sum(a.size * a.dtype.itemsize for a in operands) + sum(
        o.size * o.dtype.itemsize for o in outs
    )
    return pl.pallas_call(
        kernel,
        out_shape=outs,
        in_specs=[kinds[k] for k in places or "v" * len(operands)],
        out_specs=tuple(kinds[k] for k in out_places or "v" * len(outs)),
        scratch_shapes=scratch,
        compiler_params=pltpu.CompilerParams(vmem_limit_bytes=int(mib * 2**20)),
        cost_estimate=pl.CostEstimate(flops=flops, bytes_accessed=moved, transcendentals=0),
    )(*operands)


def exchange(blocks, axes, order):
    return lax.all_to_all(blocks, axes, 0, 0, axis_index_groups=[order])


def scan_states(chunks, place, backward, beside=None):
    shape = (chunks.shape, LOW)
    line = lax.axis_size(LINE)
    mine = exchange(chunks, PLANE, PLANE_ORDER)
    (spread,) = call(totals_kernel, [((line,) + mine.shape[1:], LOW)], mine)
    totals = exchange(spread, LINE, LINE_ORDER)
    extra = () if beside is None else tuple(beside(spread))
    order = extra[-1:]
    (low,) = call(
        functools.partial(chunks_kernel, backward), [shape], place, mine, totals, *order,
        places="svv" + "a" * len(order),
    )
    return low, extra


def on_device(queries, key_vectors, values, norm_gain, cotangent):
    rows, channels = queries.shape
    heads = channels // DH
    half = rows // 2
    members = lax.axis_size("y") * lax.axis_size("z_hi")
    plane = lax.axis_size("x") * lax.axis_size("core")
    full_width = channels * members
    place = lax.axis_index(LINE).astype(jnp.int32).reshape(1)
    gain = norm_gain.reshape(1, channels)
    unit = 2 * rows * DH * DH * heads
    chunks = ((plane, channels // plane, DH), LOW)
    whole = ((rows, channels), WIDE)
    result = ((rows, channels), LOW)
    buffer = pltpu.VMEM(*result)
    tiles = pltpu.VMEM((heads, 3 * half, half), LOW)
    sems = pltpu.SemaphoreType.DMA((2, rows // DH))

    (own,) = call(
        own_state_kernel, [chunks], place, key_vectors, values, flops=unit, places="shh",
        scratch=[buffer, buffer, pltpu.VMEM((heads, DH, DH), WIDE), sems], mib=53.6,
    )
    low, _ = scan_states(own, place, False)
    prefix_low = exchange(low, PLANE, PLANE_ORDER)
    (intra,) = call(
        intra_kernel, [whole], queries, key_vectors, values, low, flops=6 * unit,
        places="vvva", scratch=[tiles],
    )
    attended, sums = call(
        attend_kernel,
        [whole, ((members, 2 * rows // DH, DH), WIDE)],
        queries, prefix_low, intra, cotangent, gain, flops=unit,
    )
    sums = exchange(sums, HEAD, HEAD_ORDER)
    grad, own_grad, inverse = call(
        functools.partial(grad_kernel, full_width),
        [result, chunks, ((rows, DH), WIDE)],
        sums, attended, cotangent, gain, queries, flops=unit,
    )

    def products(after):
        return call(
            products_kernel,
            [result, result, whole, whole],
            grad, queries, key_vectors, values, prefix_low, attended, inverse, gain, after,
            flops=16 * unit, places="vvvvvvvva", scratch=[tiles, tiles], mib=10,
        )

    low, extra = scan_states(own_grad, place, True, products)
    query_grad, normed_out, key_part, value_part = extra
    later_low = exchange(low, PLANE, PLANE_ORDER)
    key_grad, value_grad = call(
        final_kernel,
        [result, result],
        key_vectors, values, later_low, key_part, value_part, flops=2 * unit,
        out_places="hh", scratch=[buffer, buffer, sems],
    )
    return (normed_out, query_grad, key_grad, value_grad)


def solution(mesh):
    fine = Mesh(
        mesh.devices.reshape(8, 4, 2, 4, 2), ("z_lo", "x", "core", "y", "z_hi")
    )
    placed = (P(CTX, HEAD), P(CTX, HEAD), P(CTX, HEAD), P(HEAD), P(CTX, HEAD))
    return jax.shard_map(
        on_device,
        mesh=fine,
        in_specs=placed,
        out_specs=(P(CTX, HEAD),) * 4,
        check_vma=False,
    )
```

```python
import functools

import jax
import jax.numpy as jnp
from jax import lax
from jax.experimental import pallas as pl
from jax.experimental.pallas import tpu as pltpu
from jax.sharding import Mesh, PartitionSpec as P

DH = 128
EPSILON = 1e-05
PLANE = ("x", "core")
LINE = "z_lo"
CTX = ("z_lo", "x", "core")
HEAD = ("y", "z_hi")
LINE_ORDER = [7, 6, 5, 4, 3, 2, 1, 0]
LINE_BACK_ORDER = [4, 3, 5, 2, 6, 1, 7, 0]
PLANE_ORDER = [4, 5, 6, 7, 0, 1, 2, 3]
HEAD_ORDER = [5, 7, 1, 3, 4, 6, 0, 2]
LOW = jnp.bfloat16
WIDE = jnp.float32


def dot(left, right, left_dim, right_dim):
    return lax.dot_general(
        left, right, (((left_dim,), (right_dim,)), ((), ())), preferred_element_type=WIDE
    )


def head_columns(head):
    return slice(head * DH, (head + 1) * DH)


def state_of(low_ref, head):
    rows = low_ref.shape[1]
    per_head = DH // rows
    return low_ref[head * per_head : (head + 1) * per_head].reshape(DH, DH)


def put_state(out_ref, head, state):
    rows = out_ref.shape[1]
    per_head = DH // rows
    out_ref[head * per_head : (head + 1) * per_head] = state.astype(LOW).reshape(
        per_head, rows, DH
    )


def causal_tile(size):
    return lax.broadcasted_iota(jnp.int32, (size, size), 0) >= lax.broadcasted_iota(
        jnp.int32, (size, size), 1
    )


def own_state_kernel(place_ref, left_hbm, right_hbm, out_ref, left_ref, right_ref, total_ref, sems):
    rows, channels = left_ref.shape
    copies = []
    for block in range(rows // DH):
        at = pl.ds(block * DH, DH)
        for side, (source, target) in enumerate(((left_hbm, left_ref), (right_hbm, right_ref))):
            copies.append(pltpu.make_async_copy(source.at[at], target.at[at], sems.at[side, block]))
            copies[-1].start()
    half = rows // 2
    for part in range(2):
        for copy in copies[part * len(copies) // 2 : (part + 1) * len(copies) // 2]:
            copy.wait()
        at_rows = slice(part * half, (part + 1) * half)
        for head in range(channels // DH):
            at = head_columns(head)
            state = dot(left_ref[at_rows, at], right_ref[at_rows, at], 0, 0)
            if part == 0:
                total_ref[head] = state
            else:
                put_state(out_ref, head, total_ref[head] + state)


def masked_tiles(left_ref, right_ref, at, out_ref, head):
    half = left_ref.shape[0] // 2
    causal = causal_tile(half)
    first = dot(left_ref[:, at], right_ref[:half, at], 1, 1)
    last = dot(left_ref[half:, at], right_ref[half:, at], 1, 1)
    out_ref[head, :half] = jnp.where(causal, first[:half], 0.0).astype(LOW)
    out_ref[head, half : 2 * half] = first[half:].astype(LOW)
    out_ref[head, 2 * half :] = jnp.where(causal, last, 0.0).astype(LOW)


def rows_product(tiles_ref, head, right_ref, at):
    half = tiles_ref.shape[2]
    both = dot(tiles_ref[head, : 2 * half], right_ref[:half, at], 1, 0)
    last = dot(tiles_ref[head, 2 * half :], right_ref[half:, at], 1, 0)
    return both[:half], both[half:] + last


def columns_product(tiles_ref, head, right_ref, at):
    half = tiles_ref.shape[2]
    first = dot(tiles_ref[head, : 2 * half], right_ref[:, at], 0, 0)
    last = dot(tiles_ref[head, 2 * half :], right_ref[half:, at], 0, 0)
    return first, last


def totals_kernel(mine_ref, out_ref):
    total = mine_ref[0].astype(WIDE)
    for member in range(1, mine_ref.shape[0]):
        total = total + mine_ref[member].astype(WIDE)
    out_ref[...] = jnp.broadcast_to(total.astype(LOW)[None], out_ref.shape)


def chunks_kernel(backward, place_ref, mine_ref, totals_ref, *rest):
    out_ref = rest[-1]
    place = place_ref[0]
    running = jnp.zeros(mine_ref.shape[1:], WIDE)
    for slot, plane in enumerate(LINE_BACK_ORDER if backward else LINE_ORDER):
        keep = plane > place if backward else plane < place
        running = running + jnp.where(keep, totals_ref[slot].astype(WIDE), 0.0)
    members = mine_ref.shape[0]
    for member in range(members - 1, -1, -1) if backward else range(members):
        slot = PLANE_ORDER.index(member)
        out_ref[slot] = running.astype(LOW)
        running = running + mine_ref[slot].astype(WIDE)


def attend_kernel(
    query_ref, key_ref, value_ref, low_ref, cotangent_ref, gain_ref, attended_ref, sums_ref, tiles_ref
):
    rows, channels = query_ref.shape
    half = rows // 2
    squares = [0.0, 0.0]
    slopes = [0.0, 0.0]
    for head in range(channels // DH):
        at = head_columns(head)
        masked_tiles(query_ref, key_ref, at, tiles_ref, head)
        intra = rows_product(tiles_ref, head, value_ref, at)
        inter = dot(query_ref[:, at], state_of(low_ref, head), 1, 0)
        for part in range(2):
            at_rows = slice(part * half, (part + 1) * half)
            attended = intra[part] + inter[at_rows]
            attended_ref[at_rows, at] = attended
            squares[part] = squares[part] + attended * attended
            scaled = cotangent_ref[at_rows, at].astype(WIDE) * gain_ref[:, at]
            slopes[part] = slopes[part] + scaled * attended
    parts = []
    for sums in squares + slopes:
        for block in range(half // DH):
            turned = jnp.transpose(sums[block * DH : (block + 1) * DH])
            parts.append(jnp.sum(turned, axis=0, keepdims=True))
    packed = jnp.concatenate(parts, axis=0)
    sums_ref[...] = jnp.broadcast_to(packed[None], sums_ref.shape)


def grad_kernel(
    full_width, sums_ref, attended_ref, cotangent_ref, gain_ref, query_ref,
    grad_ref, own_ref, inverse_ref,
):
    rows, channels = query_ref.shape
    blocks = rows // DH
    total = sums_ref[0]
    for member in range(1, sums_ref.shape[0]):
        total = total + sums_ref[member]
    mean = total * (1.0 / full_width)
    inverse = lax.rsqrt(mean[:blocks] + EPSILON)
    factor = inverse * inverse * inverse * mean[blocks:]
    for block in range(blocks):
        at_rows = slice(block * DH, (block + 1) * DH)
        wide = jnp.transpose(jnp.broadcast_to(inverse[block : block + 1], (DH, DH)))
        second = jnp.transpose(jnp.broadcast_to(factor[block : block + 1], (DH, DH)))
        inverse_ref[at_rows] = wide
        for head in range(channels // DH):
            at = head_columns(head)
            scaled = cotangent_ref[at_rows, at].astype(WIDE) * gain_ref[:, at]
            grad_ref[at_rows, at] = (
                wide * scaled - second * attended_ref[at_rows, at]
            ).astype(LOW)
    for head in range(channels // DH):
        at = head_columns(head)
        put_state(own_ref, head, dot(query_ref[:, at], grad_ref[:, at], 0, 0))


def products_kernel(
    grad_ref, query_ref, key_ref, value_ref, low_ref, attended_ref, inverse_ref, gain_ref, after_ref,
    query_grad_ref, normed_ref, key_part_ref, value_part_ref, tiles_ref, grad_tiles_ref,
):
    half = grad_ref.shape[0] // 2
    inverse = inverse_ref[...]
    for head in range(grad_ref.shape[1] // DH):
        at = head_columns(head)
        masked_tiles(query_ref, key_ref, at, tiles_ref, head)
        masked_tiles(grad_ref, value_ref, at, grad_tiles_ref, head)
        inter = dot(grad_ref[:, at], state_of(low_ref, head), 1, 1)
        top, bottom = rows_product(grad_tiles_ref, head, key_ref, at)
        query_grad_ref[:half, at] = (top + inter[:half]).astype(LOW)
        query_grad_ref[half:, at] = (bottom + inter[half:]).astype(LOW)
        normed_ref[:, at] = (gain_ref[:, at] * attended_ref[:, at] * inverse).astype(LOW)
        first, last = columns_product(grad_tiles_ref, head, query_ref, at)
        key_part_ref[:half, at] = first
        key_part_ref[half:, at] = last
        first, last = columns_product(tiles_ref, head, grad_ref, at)
        value_part_ref[:half, at] = first
        value_part_ref[half:, at] = last


def final_kernel(
    key_ref, value_ref, later_ref, key_part_ref, value_part_ref, key_grad_hbm, value_grad_hbm,
    key_grad_ref, value_grad_ref, sems,
):
    rows, channels = key_ref.shape
    copies = []
    for block in range(rows // DH):
        at_rows = slice(block * DH, (block + 1) * DH)
        for head in range(channels // DH):
            at = head_columns(head)
            later = state_of(later_ref, head)
            key_grad_ref[at_rows, at] = (
                key_part_ref[at_rows, at] + dot(value_ref[at_rows, at], later, 1, 1)
            ).astype(LOW)
            value_grad_ref[at_rows, at] = (
                value_part_ref[at_rows, at] + dot(key_ref[at_rows, at], later, 1, 0)
            ).astype(LOW)
        span = pl.ds(block * DH, DH)
        for side, (source, target) in enumerate(
            ((key_grad_ref, key_grad_hbm), (value_grad_ref, value_grad_hbm))
        ):
            copies.append(pltpu.make_async_copy(source.at[span], target.at[span], sems.at[side, block]))
            copies[-1].start()
    for copy in copies:
        copy.wait()


IN_VMEM = pl.BlockSpec(memory_space=pltpu.VMEM)
IN_SMEM = pl.BlockSpec(memory_space=pltpu.SMEM)
ANYWHERE = pl.BlockSpec(memory_space=pl.ANY)
IN_HBM = pl.BlockSpec(memory_space=pltpu.HBM)


def call(kernel, shapes, *operands, flops=0, places="", out_places="", scratch=(), mib=8):
    kinds = {"v": IN_VMEM, "s": IN_SMEM, "a": ANYWHERE, "h": IN_HBM}
    outs = tuple(jax.ShapeDtypeStruct(shape, kind) for shape, kind in shapes)
    moved = sum(a.size * a.dtype.itemsize for a in operands) + sum(
        o.size * o.dtype.itemsize for o in outs
    )
    return pl.pallas_call(
        kernel,
        out_shape=outs,
        in_specs=[kinds[k] for k in places or "v" * len(operands)],
        out_specs=tuple(kinds[k] for k in out_places or "v" * len(outs)),
        scratch_shapes=scratch,
        compiler_params=pltpu.CompilerParams(vmem_limit_bytes=int(mib * 2**20)),
        cost_estimate=pl.CostEstimate(flops=flops, bytes_accessed=moved, transcendentals=0),
    )(*operands)


def exchange(blocks, axes, order):
    return lax.all_to_all(blocks, axes, 0, 0, axis_index_groups=[order])


def scan_states(chunks, place, backward, beside=None):
    shape = (chunks.shape, LOW)
    line = lax.axis_size(LINE)
    mine = exchange(chunks, PLANE, PLANE_ORDER)
    (spread,) = call(totals_kernel, [((line,) + mine.shape[1:], LOW)], mine)
    totals = exchange(spread, LINE, LINE_BACK_ORDER if backward else LINE_ORDER)
    extra = () if beside is None else tuple(beside(spread))
    order = extra[-1:]
    (low,) = call(
        functools.partial(chunks_kernel, backward), [shape], place, mine, totals, *order,
        places="svv" + "a" * len(order),
    )
    return low, extra


def on_device(queries, key_vectors, values, norm_gain, cotangent):
    rows, channels = queries.shape
    heads = channels // DH
    half = rows // 2
    members = lax.axis_size("y") * lax.axis_size("z_hi")
    plane = lax.axis_size("x") * lax.axis_size("core")
    full_width = channels * members
    place = lax.axis_index(LINE).astype(jnp.int32).reshape(1)
    gain = norm_gain.reshape(1, channels)
    unit = 2 * rows * DH * DH * heads
    chunks = ((plane, channels // plane, DH), LOW)
    whole = ((rows, channels), WIDE)
    result = ((rows, channels), LOW)
    buffer = pltpu.VMEM(*result)
    tiles = pltpu.VMEM((heads, 3 * half, half), LOW)
    sems = pltpu.SemaphoreType.DMA((2, rows // DH))

    (own,) = call(
        own_state_kernel, [chunks], place, key_vectors, values, flops=unit, places="shh",
        scratch=[buffer, buffer, pltpu.VMEM((heads, DH, DH), WIDE), sems], mib=53.6,
    )
    low, _ = scan_states(own, place, False)
    prefix_low = exchange(low, PLANE, PLANE_ORDER)
    attended, sums = call(
        attend_kernel,
        [whole, ((members, 2 * rows // DH, DH), WIDE)],
        queries, key_vectors, values, prefix_low, cotangent, gain, flops=7 * unit, scratch=[tiles],
    )
    sums = exchange(sums, HEAD, HEAD_ORDER)
    grad, own_grad, inverse = call(
        functools.partial(grad_kernel, full_width),
        [result, chunks, ((rows, DH), WIDE)],
        sums, attended, cotangent, gain, queries, flops=unit,
    )

    def products(after):
        return call(
            products_kernel,
            [result, result, whole, whole],
            grad, queries, key_vectors, values, prefix_low, attended, inverse, gain, after,
            flops=16 * unit, places="vvvvvvvva", scratch=[tiles, tiles], mib=10,
        )

    low, extra = scan_states(own_grad, place, True, products)
    query_grad, normed_out, key_part, value_part = extra
    later_low = exchange(low, PLANE, PLANE_ORDER)
    key_grad, value_grad = call(
        final_kernel,
        [result, result],
        key_vectors, values, later_low, key_part, value_part, flops=2 * unit,
        out_places="hh", scratch=[buffer, buffer, sems],
    )
    return (normed_out, query_grad, key_grad, value_grad)


def solution(mesh):
    fine = Mesh(
        mesh.devices.reshape(8, 4, 2, 4, 2), ("z_lo", "x", "core", "y", "z_hi")
    )
    placed = (P(CTX, HEAD), P(CTX, HEAD), P(CTX, HEAD), P(HEAD), P(CTX, HEAD))
    return jax.shard_map(
        on_device,
        mesh=fine,
        in_specs=placed,
        out_specs=(P(CTX, HEAD),) * 4,
        check_vma=False,
    )
```

```python
import functools

import jax
import jax.numpy as jnp
from jax import lax
from jax.experimental import pallas as pl
from jax.experimental.pallas import tpu as pltpu
from jax.sharding import Mesh, PartitionSpec as P

DH = 128
EPSILON = 1e-05
PLANE = ("x", "core")
LINE = "z_lo"
CTX = ("z_lo", "x", "core")
HEAD = ("y", "z_hi")
LINE_ORDER = [4, 3, 5, 2, 6, 1, 7, 0]
PLANE_ORDER = [4, 5, 6, 7, 0, 1, 2, 3]
HEAD_ORDER = [5, 7, 1, 3, 4, 6, 0, 2]
LOW = jnp.bfloat16
WIDE = jnp.float32


def dot(left, right, left_dim, right_dim):
    return lax.dot_general(
        left, right, (((left_dim,), (right_dim,)), ((), ())), preferred_element_type=WIDE
    )


def head_columns(head):
    return slice(head * DH, (head + 1) * DH)


def state_of(low_ref, head):
    rows = low_ref.shape[1]
    per_head = DH // rows
    return low_ref[head * per_head : (head + 1) * per_head].reshape(DH, DH)


def put_state(out_ref, head, state):
    rows = out_ref.shape[1]
    per_head = DH // rows
    out_ref[head * per_head : (head + 1) * per_head] = state.astype(LOW).reshape(
        per_head, rows, DH
    )


def causal_tile(size):
    return lax.broadcasted_iota(jnp.int32, (size, size), 0) >= lax.broadcasted_iota(
        jnp.int32, (size, size), 1
    )


def own_state_kernel(place_ref, left_hbm, right_hbm, out_ref, left_ref, right_ref, total_ref, sems):
    rows, channels = left_ref.shape
    copies = []
    for block in range(rows // DH):
        at = pl.ds(block * DH, DH)
        for side, (source, target) in enumerate(((left_hbm, left_ref), (right_hbm, right_ref))):
            copies.append(pltpu.make_async_copy(source.at[at], target.at[at], sems.at[side, block]))
            copies[-1].start()
    blocks = rows // DH
    for block in range(blocks):
        for copy in copies[2 * block : 2 * block + 2]:
            copy.wait()
        at_rows = slice(block * DH, (block + 1) * DH)
        for head in range(channels // DH):
            at = head_columns(head)
            state = dot(left_ref[at_rows, at], right_ref[at_rows, at], 0, 0)
            if block > 0:
                state = total_ref[head] + state
            if block < blocks - 1:
                total_ref[head] = state
            else:
                put_state(out_ref, head, state)


def masked_tiles(left_ref, right_ref, at, out_ref, head):
    half = left_ref.shape[0] // 2
    causal = causal_tile(half)
    first = dot(left_ref[:, at], right_ref[:half, at], 1, 1)
    last = dot(left_ref[half:, at], right_ref[half:, at], 1, 1)
    out_ref[head, :half] = jnp.where(causal, first[:half], 0.0).astype(LOW)
    out_ref[head, half : 2 * half] = first[half:].astype(LOW)
    out_ref[head, 2 * half :] = jnp.where(causal, last, 0.0).astype(LOW)


def rows_product(tiles_ref, head, right_ref, at):
    half = tiles_ref.shape[2]
    both = dot(tiles_ref[head, : 2 * half], right_ref[:half, at], 1, 0)
    last = dot(tiles_ref[head, 2 * half :], right_ref[half:, at], 1, 0)
    return both[:half], both[half:] + last


def columns_product(tiles_ref, head, right_ref, at):
    half = tiles_ref.shape[2]
    first = dot(tiles_ref[head, : 2 * half], right_ref[:, at], 0, 0)
    last = dot(tiles_ref[head, 2 * half :], right_ref[half:, at], 0, 0)
    return first, last


def totals_kernel(mine_ref, out_ref):
    total = mine_ref[0].astype(WIDE)
    for member in range(1, mine_ref.shape[0]):
        total = total + mine_ref[member].astype(WIDE)
    out_ref[...] = jnp.broadcast_to(total.astype(LOW)[None], out_ref.shape)


def chunks_kernel(backward, place_ref, mine_ref, totals_ref, *rest):
    out_ref = rest[-1]
    place = place_ref[0]
    running = jnp.zeros(mine_ref.shape[1:], WIDE)
    for slot, plane in enumerate(LINE_ORDER):
        keep = plane > place if backward else plane < place
        running = running + jnp.where(keep, totals_ref[slot].astype(WIDE), 0.0)
    members = mine_ref.shape[0]
    for member in range(members - 1, -1, -1) if backward else range(members):
        slot = PLANE_ORDER.index(member)
        out_ref[slot] = running.astype(LOW)
        running = running + mine_ref[slot].astype(WIDE)


def attend_kernel(
    query_ref, key_ref, value_ref, low_ref, cotangent_ref, gain_ref, attended_ref, sums_ref, tiles_ref
):
    rows, channels = query_ref.shape
    half = rows // 2
    squares = [0.0, 0.0]
    slopes = [0.0, 0.0]
    for head in range(channels // DH):
        at = head_columns(head)
        masked_tiles(query_ref, key_ref, at, tiles_ref, head)
        intra = rows_product(tiles_ref, head, value_ref, at)
        inter = dot(query_ref[:, at], state_of(low_ref, head), 1, 0)
        for part in range(2):
            at_rows = slice(part * half, (part + 1) * half)
            attended = intra[part] + inter[at_rows]
            attended_ref[at_rows, at] = attended
            squares[part] = squares[part] + attended * attended
            scaled = cotangent_ref[at_rows, at].astype(WIDE) * gain_ref[:, at]
            slopes[part] = slopes[part] + scaled * attended
    parts = []
    for sums in squares + slopes:
        for block in range(half // DH):
            turned = jnp.transpose(sums[block * DH : (block + 1) * DH])
            parts.append(jnp.sum(turned, axis=0, keepdims=True))
    packed = jnp.concatenate(parts, axis=0)
    sums_ref[...] = jnp.broadcast_to(packed[None], sums_ref.shape)


def grad_kernel(
    full_width, sums_ref, attended_ref, cotangent_ref, gain_ref, query_ref,
    grad_ref, own_ref, inverse_ref,
):
    rows, channels = query_ref.shape
    blocks = rows // DH
    total = sums_ref[0]
    for member in range(1, sums_ref.shape[0]):
        total = total + sums_ref[member]
    mean = total * (1.0 / full_width)
    inverse = lax.rsqrt(mean[:blocks] + EPSILON)
    factor = inverse * inverse * inverse * mean[blocks:]
    for block in range(blocks):
        at_rows = slice(block * DH, (block + 1) * DH)
        wide = jnp.transpose(jnp.broadcast_to(inverse[block : block + 1], (DH, DH)))
        second = jnp.transpose(jnp.broadcast_to(factor[block : block + 1], (DH, DH)))
        inverse_ref[at_rows] = wide
        for head in range(channels // DH):
            at = head_columns(head)
            scaled = cotangent_ref[at_rows, at].astype(WIDE) * gain_ref[:, at]
            grad_ref[at_rows, at] = (
                wide * scaled - second * attended_ref[at_rows, at]
            ).astype(LOW)
    for head in range(channels // DH):
        at = head_columns(head)
        put_state(own_ref, head, dot(query_ref[:, at], grad_ref[:, at], 0, 0))


def products_kernel(
    grad_ref, query_ref, key_ref, value_ref, low_ref, attended_ref, inverse_ref, gain_ref, after_ref,
    query_grad_ref, normed_ref, key_part_ref, value_part_ref, tiles_ref, grad_tiles_ref,
):
    half = grad_ref.shape[0] // 2
    inverse = inverse_ref[...]
    for head in range(grad_ref.shape[1] // DH):
        at = head_columns(head)
        masked_tiles(query_ref, key_ref, at, tiles_ref, head)
        masked_tiles(grad_ref, value_ref, at, grad_tiles_ref, head)
        inter = dot(grad_ref[:, at], state_of(low_ref, head), 1, 1)
        top, bottom = rows_product(grad_tiles_ref, head, key_ref, at)
        query_grad_ref[:half, at] = (top + inter[:half]).astype(LOW)
        query_grad_ref[half:, at] = (bottom + inter[half:]).astype(LOW)
        normed_ref[:, at] = (gain_ref[:, at] * attended_ref[:, at] * inverse).astype(LOW)
        first, last = columns_product(grad_tiles_ref, head, query_ref, at)
        key_part_ref[:half, at] = first
        key_part_ref[half:, at] = last
        first, last = columns_product(tiles_ref, head, grad_ref, at)
        value_part_ref[:half, at] = first
        value_part_ref[half:, at] = last


def final_kernel(
    key_ref, value_ref, later_ref, key_part_ref, value_part_ref, key_grad_hbm, value_grad_hbm,
    key_grad_ref, value_grad_ref, sems,
):
    rows, channels = key_ref.shape
    copies = []
    step = rows // 2
    for block in range(2):
        at_rows = slice(block * step, (block + 1) * step)
        for head in range(channels // DH):
            at = head_columns(head)
            later = state_of(later_ref, head)
            key_grad_ref[at_rows, at] = (
                key_part_ref[at_rows, at] + dot(value_ref[at_rows, at], later, 1, 1)
            ).astype(LOW)
            value_grad_ref[at_rows, at] = (
                value_part_ref[at_rows, at] + dot(key_ref[at_rows, at], later, 1, 0)
            ).astype(LOW)
        span = pl.ds(block * step, step)
        for side, (source, target) in enumerate(
            ((key_grad_ref, key_grad_hbm), (value_grad_ref, value_grad_hbm))
        ):
            copies.append(pltpu.make_async_copy(source.at[span], target.at[span], sems.at[side, block]))
            copies[-1].start()
    for copy in copies:
        copy.wait()


IN_VMEM = pl.BlockSpec(memory_space=pltpu.VMEM)
IN_SMEM = pl.BlockSpec(memory_space=pltpu.SMEM)
ANYWHERE = pl.BlockSpec(memory_space=pl.ANY)
IN_HBM = pl.BlockSpec(memory_space=pltpu.HBM)


def call(kernel, shapes, *operands, flops=0, places="", out_places="", scratch=(), mib=8):
    kinds = {"v": IN_VMEM, "s": IN_SMEM, "a": ANYWHERE, "h": IN_HBM}
    outs = tuple(jax.ShapeDtypeStruct(shape, kind) for shape, kind in shapes)
    moved = sum(a.size * a.dtype.itemsize for a in operands) + sum(
        o.size * o.dtype.itemsize for o in outs
    )
    return pl.pallas_call(
        kernel,
        out_shape=outs,
        in_specs=[kinds[k] for k in places or "v" * len(operands)],
        out_specs=tuple(kinds[k] for k in out_places or "v" * len(outs)),
        scratch_shapes=scratch,
        compiler_params=pltpu.CompilerParams(vmem_limit_bytes=int(mib * 2**20)),
        cost_estimate=pl.CostEstimate(flops=flops, bytes_accessed=moved, transcendentals=0),
    )(*operands)


def exchange(blocks, axes, order):
    return lax.all_to_all(blocks, axes, 0, 0, axis_index_groups=[order])


def scan_states(chunks, place, backward, beside=None):
    shape = (chunks.shape, LOW)
    line = lax.axis_size(LINE)
    mine = exchange(chunks, PLANE, PLANE_ORDER)
    (spread,) = call(totals_kernel, [((line,) + mine.shape[1:], LOW)], mine)
    totals = exchange(spread, LINE, LINE_ORDER)
    extra = () if beside is None else tuple(beside(spread))
    order = extra[-1:]
    (low,) = call(
        functools.partial(chunks_kernel, backward), [shape], place, mine, totals, *order,
        places="svv" + "a" * len(order),
    )
    return low, extra


def on_device(queries, key_vectors, values, norm_gain, cotangent):
    rows, channels = queries.shape
    heads = channels // DH
    half = rows // 2
    members = lax.axis_size("y") * lax.axis_size("z_hi")
    plane = lax.axis_size("x") * lax.axis_size("core")
    full_width = channels * members
    place = lax.axis_index(LINE).astype(jnp.int32).reshape(1)
    gain = norm_gain.reshape(1, channels)
    unit = 2 * rows * DH * DH * heads
    chunks = ((plane, channels // plane, DH), LOW)
    whole = ((rows, channels), WIDE)
    result = ((rows, channels), LOW)
    buffer = pltpu.VMEM(*result)
    tiles = pltpu.VMEM((heads, 3 * half, half), LOW)
    sems = pltpu.SemaphoreType.DMA((2, rows // DH))

    (own,) = call(
        own_state_kernel, [chunks], place, key_vectors, values, flops=unit, places="shh",
        scratch=[buffer, buffer, pltpu.VMEM((heads, DH, DH), WIDE), sems], mib=53.6,
    )
    low, _ = scan_states(own, place, False)
    prefix_low = exchange(low, PLANE, PLANE_ORDER)
    attended, sums = call(
        attend_kernel,
        [whole, ((members, 2 * rows // DH, DH), WIDE)],
        queries, key_vectors, values, prefix_low, cotangent, gain, flops=7 * unit, scratch=[tiles],
    )
    sums = exchange(sums, HEAD, HEAD_ORDER)
    grad, own_grad, inverse = call(
        functools.partial(grad_kernel, full_width),
        [result, chunks, ((rows, DH), WIDE)],
        sums, attended, cotangent, gain, queries, flops=unit,
    )

    def products(after):
        return call(
            products_kernel,
            [result, result, whole, whole],
            grad, queries, key_vectors, values, prefix_low, attended, inverse, gain, after,
            flops=16 * unit, places="vvvvvvvva", scratch=[tiles, tiles], mib=10,
        )

    low, extra = scan_states(own_grad, place, True, products)
    query_grad, normed_out, key_part, value_part = extra
    later_low = exchange(low, PLANE, PLANE_ORDER)
    key_grad, value_grad = call(
        final_kernel,
        [result, result],
        key_vectors, values, later_low, key_part, value_part, flops=2 * unit,
        out_places="hh", scratch=[buffer, buffer, sems],
    )
    return (normed_out, query_grad, key_grad, value_grad)


def solution(mesh):
    fine = Mesh(
        mesh.devices.reshape(8, 4, 2, 4, 2), ("z_lo", "x", "core", "y", "z_hi")
    )
    placed = (P(CTX, HEAD), P(CTX, HEAD), P(CTX, HEAD), P(HEAD), P(CTX, HEAD))
    return jax.shard_map(
        on_device,
        mesh=fine,
        in_specs=placed,
        out_specs=(P(CTX, HEAD),) * 4,
        check_vma=False,
    )
```

```python
import functools

import jax
import jax.numpy as jnp
from jax import lax
from jax.experimental import pallas as pl
from jax.experimental.pallas import tpu as pltpu
from jax.sharding import Mesh, PartitionSpec as P

DH = 128
EPSILON = 1e-05
PLANE = ("x", "core")
LINE = "z_lo"
CTX = ("z_lo", "x", "core")
HEAD = ("y", "z_hi")
LINE_ORDER = [4, 5, 6, 7, 0, 1, 2, 3]
PLANE_ORDER = [5, 1, 0, 4, 7, 6, 3, 2]
HEAD_ORDER = [5, 7, 1, 3, 4, 6, 0, 2]
LOW = jnp.bfloat16
WIDE = jnp.float32


def dot(left, right, left_dim, right_dim):
    return lax.dot_general(
        left, right, (((left_dim,), (right_dim,)), ((), ())), preferred_element_type=WIDE
    )


def head_columns(head):
    return slice(head * DH, (head + 1) * DH)


def state_of(low_ref, head):
    rows = low_ref.shape[1]
    per_head = DH // rows
    return low_ref[head * per_head : (head + 1) * per_head].reshape(DH, DH)


def put_state(out_ref, head, state):
    rows = out_ref.shape[1]
    per_head = DH // rows
    out_ref[head * per_head : (head + 1) * per_head] = state.astype(LOW).reshape(
        per_head, rows, DH
    )


def causal_tile(size):
    return lax.broadcasted_iota(jnp.int32, (size, size), 0) >= lax.broadcasted_iota(
        jnp.int32, (size, size), 1
    )


def own_state_kernel(place_ref, left_hbm, right_hbm, out_ref, left_ref, right_ref, total_ref, sems):
    rows, channels = left_ref.shape
    copies = []
    for block in range(rows // DH):
        at = pl.ds(block * DH, DH)
        for side, (source, target) in enumerate(((left_hbm, left_ref), (right_hbm, right_ref))):
            copies.append(pltpu.make_async_copy(source.at[at], target.at[at], sems.at[side, block]))
            copies[-1].start()
    blocks = rows // DH
    for block in range(blocks):
        for copy in copies[2 * block : 2 * block + 2]:
            copy.wait()
        at_rows = slice(block * DH, (block + 1) * DH)
        for head in range(channels // DH):
            at = head_columns(head)
            state = dot(left_ref[at_rows, at], right_ref[at_rows, at], 0, 0)
            if block > 0:
                state = total_ref[head] + state
            if block < blocks - 1:
                total_ref[head] = state
            else:
                put_state(out_ref, head, state)


def masked_tiles(left_ref, right_ref, at, out_ref, head):
    half = left_ref.shape[0] // 2
    causal = causal_tile(half)
    first = dot(left_ref[:, at], right_ref[:half, at], 1, 1)
    last = dot(left_ref[half:, at], right_ref[half:, at], 1, 1)
    out_ref[head, :half] = jnp.where(causal, first[:half], 0.0).astype(LOW)
    out_ref[head, half : 2 * half] = first[half:].astype(LOW)
    out_ref[head, 2 * half :] = jnp.where(causal, last, 0.0).astype(LOW)


def rows_product(tiles_ref, head, right_ref, at):
    half = tiles_ref.shape[2]
    both = dot(tiles_ref[head, : 2 * half], right_ref[:half, at], 1, 0)
    last = dot(tiles_ref[head, 2 * half :], right_ref[half:, at], 1, 0)
    return both[:half], both[half:] + last


def columns_product(tiles_ref, head, right_ref, at):
    half = tiles_ref.shape[2]
    first = dot(tiles_ref[head, : 2 * half], right_ref[:, at], 0, 0)
    last = dot(tiles_ref[head, 2 * half :], right_ref[half:, at], 0, 0)
    return first, last


def totals_kernel(mine_ref, out_ref):
    total = mine_ref[0].astype(WIDE)
    for member in range(1, mine_ref.shape[0]):
        total = total + mine_ref[member].astype(WIDE)
    out_ref[...] = jnp.broadcast_to(total.astype(LOW)[None], out_ref.shape)


def chunks_kernel(backward, place_ref, mine_ref, totals_ref, *rest):
    out_ref = rest[-1]
    place = place_ref[0]
    running = jnp.zeros(mine_ref.shape[1:], WIDE)
    for slot, plane in enumerate(LINE_ORDER):
        keep = plane > place if backward else plane < place
        running = running + jnp.where(keep, totals_ref[slot].astype(WIDE), 0.0)
    members = mine_ref.shape[0]
    for member in range(members - 1, -1, -1) if backward else range(members):
        slot = PLANE_ORDER.index(member)
        out_ref[slot] = running.astype(LOW)
        running = running + mine_ref[slot].astype(WIDE)


def attend_kernel(
    query_ref, key_ref, value_ref, low_ref, cotangent_ref, gain_ref, attended_ref, sums_ref
):
    rows, channels = query_ref.shape
    half = rows // 2
    causal = causal_tile(half)
    squares = [0.0, 0.0]
    slopes = [0.0, 0.0]
    for head in range(channels // DH):
        at = head_columns(head)
        first = dot(query_ref[:, at], key_ref[:half, at], 1, 1)
        last = dot(query_ref[half:, at], key_ref[half:, at], 1, 1)
        left = jnp.concatenate([jnp.where(causal, first[:half], 0.0), first[half:]]).astype(LOW)
        left = dot(left, value_ref[:half, at], 1, 0)
        last = jnp.where(causal, last, 0.0).astype(LOW)
        intra = left[:half], left[half:] + dot(last, value_ref[half:, at], 1, 0)
        inter = dot(query_ref[:, at], state_of(low_ref, head), 1, 0)
        for part in range(2):
            at_rows = slice(part * half, (part + 1) * half)
            attended = intra[part] + inter[at_rows]
            attended_ref[at_rows, at] = attended
            squares[part] = squares[part] + attended * attended
            scaled = cotangent_ref[at_rows, at].astype(WIDE) * gain_ref[:, at]
            slopes[part] = slopes[part] + scaled * attended
    parts = []
    for sums in squares + slopes:
        for block in range(half // DH):
            turned = jnp.transpose(sums[block * DH : (block + 1) * DH])
            parts.append(jnp.sum(turned, axis=0, keepdims=True))
    packed = jnp.concatenate(parts, axis=0)
    sums_ref[...] = jnp.broadcast_to(packed[None], sums_ref.shape)


def grad_kernel(
    full_width, sums_ref, attended_ref, cotangent_ref, gain_ref, query_ref,
    grad_ref, own_ref, inverse_ref,
):
    rows, channels = query_ref.shape
    blocks = rows // DH
    total = sums_ref[0]
    for member in range(1, sums_ref.shape[0]):
        total = total + sums_ref[member]
    mean = total * (1.0 / full_width)
    inverse = lax.rsqrt(mean[:blocks] + EPSILON)
    factor = inverse * inverse * inverse * mean[blocks:]
    for block in range(blocks):
        at_rows = slice(block * DH, (block + 1) * DH)
        wide = jnp.transpose(jnp.broadcast_to(inverse[block : block + 1], (DH, DH)))
        second = jnp.transpose(jnp.broadcast_to(factor[block : block + 1], (DH, DH)))
        inverse_ref[at_rows] = wide
        for head in range(channels // DH):
            at = head_columns(head)
            scaled = cotangent_ref[at_rows, at].astype(WIDE) * gain_ref[:, at]
            grad_ref[at_rows, at] = (
                wide * scaled - second * attended_ref[at_rows, at]
            ).astype(LOW)
    for head in range(channels // DH):
        at = head_columns(head)
        put_state(own_ref, head, dot(query_ref[:, at], grad_ref[:, at], 0, 0))


def products_kernel(
    grad_ref, query_ref, key_ref, value_ref, low_ref, attended_ref, inverse_ref, gain_ref, after_ref,
    query_grad_ref, normed_ref, key_part_ref, value_part_ref, tiles_ref, grad_tiles_ref,
):
    half = grad_ref.shape[0] // 2
    inverse = inverse_ref[...]
    for head in range(grad_ref.shape[1] // DH):
        at = head_columns(head)
        masked_tiles(query_ref, key_ref, at, tiles_ref, head)
        masked_tiles(grad_ref, value_ref, at, grad_tiles_ref, head)
        inter = dot(grad_ref[:, at], state_of(low_ref, head), 1, 1)
        top, bottom = rows_product(grad_tiles_ref, head, key_ref, at)
        query_grad_ref[:half, at] = (top + inter[:half]).astype(LOW)
        query_grad_ref[half:, at] = (bottom + inter[half:]).astype(LOW)
        normed_ref[:, at] = (gain_ref[:, at] * attended_ref[:, at] * inverse).astype(LOW)
        first, last = columns_product(grad_tiles_ref, head, query_ref, at)
        key_part_ref[:half, at] = first
        key_part_ref[half:, at] = last
        first, last = columns_product(tiles_ref, head, grad_ref, at)
        value_part_ref[:half, at] = first
        value_part_ref[half:, at] = last


def final_kernel(
    key_ref, value_ref, later_ref, key_part_ref, value_part_ref, key_grad_hbm, value_grad_hbm,
    key_grad_ref, value_grad_ref, sems,
):
    rows, channels = key_ref.shape
    copies = []
    step = rows // 2
    for block in range(2):
        at_rows = slice(block * step, (block + 1) * step)
        for head in range(channels // DH):
            at = head_columns(head)
            later = state_of(later_ref, head)
            key_grad_ref[at_rows, at] = (
                key_part_ref[at_rows, at] + dot(value_ref[at_rows, at], later, 1, 1)
            ).astype(LOW)
            value_grad_ref[at_rows, at] = (
                value_part_ref[at_rows, at] + dot(key_ref[at_rows, at], later, 1, 0)
            ).astype(LOW)
        span = pl.ds(block * step, step)
        for side, (source, target) in enumerate(
            ((key_grad_ref, key_grad_hbm), (value_grad_ref, value_grad_hbm))
        ):
            copies.append(pltpu.make_async_copy(source.at[span], target.at[span], sems.at[side, block]))
            copies[-1].start()
    for copy in copies:
        copy.wait()


IN_VMEM = pl.BlockSpec(memory_space=pltpu.VMEM)
IN_SMEM = pl.BlockSpec(memory_space=pltpu.SMEM)
ANYWHERE = pl.BlockSpec(memory_space=pl.ANY)
IN_HBM = pl.BlockSpec(memory_space=pltpu.HBM)


def call(kernel, shapes, *operands, flops=0, places="", out_places="", scratch=(), mib=8):
    kinds = {"v": IN_VMEM, "s": IN_SMEM, "a": ANYWHERE, "h": IN_HBM}
    outs = tuple(jax.ShapeDtypeStruct(shape, kind) for shape, kind in shapes)
    moved = sum(a.size * a.dtype.itemsize for a in operands) + sum(
        o.size * o.dtype.itemsize for o in outs
    )
    return pl.pallas_call(
        kernel,
        out_shape=outs,
        in_specs=[kinds[k] for k in places or "v" * len(operands)],
        out_specs=tuple(kinds[k] for k in out_places or "v" * len(outs)),
        scratch_shapes=scratch,
        compiler_params=pltpu.CompilerParams(vmem_limit_bytes=int(mib * 2**20)),
        cost_estimate=pl.CostEstimate(flops=flops, bytes_accessed=moved, transcendentals=0),
    )(*operands)


def exchange(blocks, axes, order):
    return lax.all_to_all(blocks, axes, 0, 0, axis_index_groups=[order])


def scan_states(chunks, place, backward, beside=None):
    shape = (chunks.shape, LOW)
    line = lax.axis_size(LINE)
    mine = exchange(chunks, PLANE, PLANE_ORDER)
    (spread,) = call(totals_kernel, [((line,) + mine.shape[1:], LOW)], mine)
    totals = exchange(spread, LINE, LINE_ORDER)
    extra = () if beside is None else tuple(beside(spread))
    order = extra[-1:]
    (low,) = call(
        functools.partial(chunks_kernel, backward), [shape], place, mine, totals, *order,
        places="svv" + "a" * len(order),
    )
    return low, extra


def on_device(queries, key_vectors, values, norm_gain, cotangent):
    rows, channels = queries.shape
    heads = channels // DH
    half = rows // 2
    members = lax.axis_size("y") * lax.axis_size("z_hi")
    plane = lax.axis_size("x") * lax.axis_size("core")
    full_width = channels * members
    place = lax.axis_index(LINE).astype(jnp.int32).reshape(1)
    gain = norm_gain.reshape(1, channels)
    unit = 2 * rows * DH * DH * heads
    chunks = ((plane, channels // plane, DH), LOW)
    whole = ((rows, channels), WIDE)
    result = ((rows, channels), LOW)
    buffer = pltpu.VMEM(*result)
    tiles = pltpu.VMEM((heads, 3 * half, half), LOW)
    sems = pltpu.SemaphoreType.DMA((2, rows // DH))

    (own,) = call(
        own_state_kernel, [chunks], place, key_vectors, values, flops=unit, places="shh",
        scratch=[buffer, buffer, pltpu.VMEM((heads, DH, DH), WIDE), sems], mib=53.6,
    )
    low, _ = scan_states(own, place, False)
    prefix_low = exchange(low, PLANE, PLANE_ORDER)
    attended, sums = call(
        attend_kernel,
        [whole, ((members, 2 * rows // DH, DH), WIDE)],
        queries, key_vectors, values, prefix_low, cotangent, gain, flops=7 * unit,
    )
    sums = exchange(sums, HEAD, HEAD_ORDER)
    grad, own_grad, inverse = call(
        functools.partial(grad_kernel, full_width),
        [result, chunks, ((rows, DH), WIDE)],
        sums, attended, cotangent, gain, queries, flops=unit,
    )

    def products(after):
        return call(
            products_kernel,
            [result, result, whole, whole],
            grad, queries, key_vectors, values, prefix_low, attended, inverse, gain, after,
            flops=16 * unit, places="vvvvvvvva", scratch=[tiles, tiles], mib=10,
        )

    low, extra = scan_states(own_grad, place, True, products)
    query_grad, normed_out, key_part, value_part = extra
    later_low = exchange(low, PLANE, PLANE_ORDER)
    key_grad, value_grad = call(
        final_kernel,
        [result, result],
        key_vectors, values, later_low, key_part, value_part, flops=2 * unit,
        out_places="hh", scratch=[buffer, buffer, sems],
    )
    return (normed_out, query_grad, key_grad, value_grad)


def solution(mesh):
    fine = Mesh(
        mesh.devices.reshape(8, 4, 2, 4, 2), ("z_lo", "x", "core", "y", "z_hi")
    )
    placed = (P(CTX, HEAD), P(CTX, HEAD), P(CTX, HEAD), P(HEAD), P(CTX, HEAD))
    return jax.shard_map(
        on_device,
        mesh=fine,
        in_specs=placed,
        out_specs=(P(CTX, HEAD),) * 4,
        check_vma=False,
    )
```

```python
import functools

import jax
import jax.numpy as jnp
from jax import lax
from jax.experimental import pallas as pl
from jax.experimental.pallas import tpu as pltpu
from jax.sharding import Mesh, PartitionSpec as P

DH = 128
EPSILON = 1e-05
PLANE = ("x", "core")
LINE = "z_lo"
CTX = ("z_lo", "x", "core")
HEAD = ("y", "z_hi")
LINE_ORDER = [4, 5, 6, 7, 0, 1, 2, 3]
PLANE_ORDER = [5, 1, 0, 4, 7, 6, 3, 2]
HEAD_ORDER = [5, 7, 1, 3, 4, 6, 0, 2]
LOW = jnp.bfloat16
WIDE = jnp.float32


def dot(left, right, left_dim, right_dim):
    return lax.dot_general(
        left, right, (((left_dim,), (right_dim,)), ((), ())), preferred_element_type=WIDE
    )


def head_columns(head):
    return slice(head * DH, (head + 1) * DH)


def state_of(low_ref, head):
    rows = low_ref.shape[1]
    per_head = DH // rows
    return low_ref[head * per_head : (head + 1) * per_head].reshape(DH, DH)


def put_state(out_ref, head, state):
    rows = out_ref.shape[1]
    per_head = DH // rows
    out_ref[head * per_head : (head + 1) * per_head] = state.astype(LOW).reshape(
        per_head, rows, DH
    )


def causal_tile(size):
    return lax.broadcasted_iota(jnp.int32, (size, size), 0) >= lax.broadcasted_iota(
        jnp.int32, (size, size), 1
    )


def own_state_kernel(place_ref, left_hbm, right_hbm, out_ref, left_ref, right_ref, total_ref, sems):
    rows, channels = left_ref.shape
    copies = []
    for block in range(rows // DH):
        at = pl.ds(block * DH, DH)
        for side, (source, target) in enumerate(((left_hbm, left_ref), (right_hbm, right_ref))):
            copies.append(pltpu.make_async_copy(source.at[at], target.at[at], sems.at[side, block]))
            copies[-1].start()
    blocks = rows // DH
    for block in range(blocks):
        for copy in copies[2 * block : 2 * block + 2]:
            copy.wait()
        at_rows = slice(block * DH, (block + 1) * DH)
        for head in range(channels // DH):
            at = head_columns(head)
            state = dot(left_ref[at_rows, at], right_ref[at_rows, at], 0, 0)
            if block > 0:
                state = total_ref[head] + state
            if block < blocks - 1:
                total_ref[head] = state
            else:
                put_state(out_ref, head, state)


def masked_tiles(left_ref, right_ref, at, out_ref, head):
    half = left_ref.shape[0] // 2
    causal = causal_tile(half)
    first = dot(left_ref[:, at], right_ref[:half, at], 1, 1)
    last = dot(left_ref[half:, at], right_ref[half:, at], 1, 1)
    out_ref[head, :half] = jnp.where(causal, first[:half], 0.0).astype(LOW)
    out_ref[head, half : 2 * half] = first[half:].astype(LOW)
    out_ref[head, 2 * half :] = jnp.where(causal, last, 0.0).astype(LOW)


def rows_product(tiles_ref, head, right_ref, at):
    half = tiles_ref.shape[2]
    both = dot(tiles_ref[head, : 2 * half], right_ref[:half, at], 1, 0)
    last = dot(tiles_ref[head, 2 * half :], right_ref[half:, at], 1, 0)
    return both[:half], both[half:] + last


def columns_product(tiles_ref, head, right_ref, at):
    half = tiles_ref.shape[2]
    first = dot(tiles_ref[head, : 2 * half], right_ref[:, at], 0, 0)
    last = dot(tiles_ref[head, 2 * half :], right_ref[half:, at], 0, 0)
    return first, last


def totals_kernel(mine_ref, out_ref):
    total = mine_ref[0].astype(WIDE)
    for member in range(1, mine_ref.shape[0]):
        total = total + mine_ref[member].astype(WIDE)
    out_ref[...] = jnp.broadcast_to(total.astype(LOW)[None], out_ref.shape)


def chunks_kernel(backward, place_ref, mine_ref, totals_ref, *rest):
    out_ref = rest[-1]
    place = place_ref[0]
    running = jnp.zeros(mine_ref.shape[1:], WIDE)
    for slot, plane in enumerate(LINE_ORDER):
        keep = plane > place if backward else plane < place
        running = running + jnp.where(keep, totals_ref[slot].astype(WIDE), 0.0)
    members = mine_ref.shape[0]
    for member in range(members - 1, -1, -1) if backward else range(members):
        slot = PLANE_ORDER.index(member)
        out_ref[slot] = running.astype(LOW)
        running = running + mine_ref[slot].astype(WIDE)


def attend_kernel(
    query_ref, key_ref, value_ref, low_ref, cotangent_ref, gain_ref, attended_ref, sums_ref
):
    rows, channels = query_ref.shape
    half = rows // 2
    causal = causal_tile(half)
    squares = [0.0, 0.0]
    slopes = [0.0, 0.0]
    for head in range(channels // DH):
        at = head_columns(head)
        first = dot(query_ref[:, at], key_ref[:half, at], 1, 1)
        last = dot(query_ref[half:, at], key_ref[half:, at], 1, 1)
        left = jnp.concatenate([jnp.where(causal, first[:half], 0.0), first[half:]]).astype(LOW)
        left = dot(left, value_ref[:half, at], 1, 0)
        last = jnp.where(causal, last, 0.0).astype(LOW)
        intra = left[:half], left[half:] + dot(last, value_ref[half:, at], 1, 0)
        inter = dot(query_ref[:, at], state_of(low_ref, head), 1, 0)
        for part in range(2):
            at_rows = slice(part * half, (part + 1) * half)
            attended = intra[part] + inter[at_rows]
            attended_ref[at_rows, at] = attended
            squares[part] = squares[part] + attended * attended
            scaled = cotangent_ref[at_rows, at].astype(WIDE) * gain_ref[:, at]
            slopes[part] = slopes[part] + scaled * attended
    parts = []
    for sums in squares + slopes:
        for block in range(half // DH):
            turned = jnp.transpose(sums[block * DH : (block + 1) * DH])
            parts.append(jnp.sum(turned, axis=0, keepdims=True))
    packed = jnp.concatenate(parts, axis=0)
    sums_ref[...] = jnp.broadcast_to(packed[None], sums_ref.shape)


def grad_kernel(
    full_width, sums_ref, attended_ref, cotangent_ref, gain_ref, query_ref,
    grad_ref, own_ref, inverse_ref,
):
    rows, channels = query_ref.shape
    blocks = rows // DH
    total = sums_ref[0]
    for member in range(1, sums_ref.shape[0]):
        total = total + sums_ref[member]
    mean = total * (1.0 / full_width)
    inverse = lax.rsqrt(mean[:blocks] + EPSILON)
    factor = inverse * inverse * inverse * mean[blocks:]
    inverse_ref[...] = inverse
    for block in range(blocks):
        at_rows = slice(block * DH, (block + 1) * DH)
        wide = jnp.transpose(jnp.broadcast_to(inverse[block : block + 1], (DH, DH)))
        second = jnp.transpose(jnp.broadcast_to(factor[block : block + 1], (DH, DH)))
        for head in range(channels // DH):
            at = head_columns(head)
            scaled = cotangent_ref[at_rows, at].astype(WIDE) * gain_ref[:, at]
            grad_ref[at_rows, at] = (
                wide * scaled - second * attended_ref[at_rows, at]
            ).astype(LOW)
    for head in range(channels // DH):
        at = head_columns(head)
        put_state(own_ref, head, dot(query_ref[:, at], grad_ref[:, at], 0, 0))


def products_kernel(
    grad_ref, query_ref, key_ref, value_ref, low_ref, attended_ref, inverse_ref, gain_ref, after_ref,
    query_grad_ref, normed_ref, key_part_ref, value_part_ref, tiles_ref, grad_tiles_ref,
):
    half = grad_ref.shape[0] // 2
    turned = []
    for block in range(inverse_ref.shape[0]):
        turned.append(jnp.transpose(jnp.broadcast_to(inverse_ref[block : block + 1], (DH, DH))))
    inverse = jnp.concatenate(turned, axis=0)
    for head in range(grad_ref.shape[1] // DH):
        at = head_columns(head)
        masked_tiles(query_ref, key_ref, at, tiles_ref, head)
        masked_tiles(grad_ref, value_ref, at, grad_tiles_ref, head)
        inter = dot(grad_ref[:, at], state_of(low_ref, head), 1, 1)
        top, bottom = rows_product(grad_tiles_ref, head, key_ref, at)
        query_grad_ref[:half, at] = (top + inter[:half]).astype(LOW)
        query_grad_ref[half:, at] = (bottom + inter[half:]).astype(LOW)
        normed_ref[:, at] = (gain_ref[:, at] * attended_ref[:, at] * inverse).astype(LOW)
        first, last = columns_product(grad_tiles_ref, head, query_ref, at)
        key_part_ref[:half, at] = first
        key_part_ref[half:, at] = last
        first, last = columns_product(tiles_ref, head, grad_ref, at)
        value_part_ref[:half, at] = first
        value_part_ref[half:, at] = last


def final_kernel(
    key_ref, value_ref, later_ref, key_part_ref, value_part_ref, key_grad_hbm, value_grad_hbm,
    key_grad_ref, value_grad_ref, sems,
):
    rows, channels = key_ref.shape
    copies = []
    step = rows // 2
    for block in range(2):
        at_rows = slice(block * step, (block + 1) * step)
        for head in range(channels // DH):
            at = head_columns(head)
            later = state_of(later_ref, head)
            key_grad_ref[at_rows, at] = (
                key_part_ref[at_rows, at] + dot(value_ref[at_rows, at], later, 1, 1)
            ).astype(LOW)
            value_grad_ref[at_rows, at] = (
                value_part_ref[at_rows, at] + dot(key_ref[at_rows, at], later, 1, 0)
            ).astype(LOW)
        span = pl.ds(block * step, step)
        for side, (source, target) in enumerate(
            ((key_grad_ref, key_grad_hbm), (value_grad_ref, value_grad_hbm))
        ):
            copies.append(pltpu.make_async_copy(source.at[span], target.at[span], sems.at[side, block]))
            copies[-1].start()
    for copy in copies:
        copy.wait()


IN_VMEM = pl.BlockSpec(memory_space=pltpu.VMEM)
IN_SMEM = pl.BlockSpec(memory_space=pltpu.SMEM)
ANYWHERE = pl.BlockSpec(memory_space=pl.ANY)
IN_HBM = pl.BlockSpec(memory_space=pltpu.HBM)


def call(kernel, shapes, *operands, flops=0, places="", out_places="", scratch=(), mib=8):
    kinds = {"v": IN_VMEM, "s": IN_SMEM, "a": ANYWHERE, "h": IN_HBM}
    outs = tuple(jax.ShapeDtypeStruct(shape, kind) for shape, kind in shapes)
    moved = sum(a.size * a.dtype.itemsize for a in operands) + sum(
        o.size * o.dtype.itemsize for o in outs
    )
    return pl.pallas_call(
        kernel,
        out_shape=outs,
        in_specs=[kinds[k] for k in places or "v" * len(operands)],
        out_specs=tuple(kinds[k] for k in out_places or "v" * len(outs)),
        scratch_shapes=scratch,
        compiler_params=pltpu.CompilerParams(vmem_limit_bytes=int(mib * 2**20)),
        cost_estimate=pl.CostEstimate(flops=flops, bytes_accessed=moved, transcendentals=0),
    )(*operands)


def exchange(blocks, axes, order):
    return lax.all_to_all(blocks, axes, 0, 0, axis_index_groups=[order])


def scan_states(chunks, place, backward, beside=None):
    shape = (chunks.shape, LOW)
    line = lax.axis_size(LINE)
    mine = exchange(chunks, PLANE, PLANE_ORDER)
    (spread,) = call(totals_kernel, [((line,) + mine.shape[1:], LOW)], mine)
    totals = exchange(spread, LINE, LINE_ORDER)
    extra = () if beside is None else tuple(beside(spread))
    order = extra[-1:]
    (low,) = call(
        functools.partial(chunks_kernel, backward), [shape], place, mine, totals, *order,
        places="svv" + "a" * len(order),
    )
    return low, extra


def on_device(queries, key_vectors, values, norm_gain, cotangent):
    rows, channels = queries.shape
    heads = channels // DH
    half = rows // 2
    members = lax.axis_size("y") * lax.axis_size("z_hi")
    plane = lax.axis_size("x") * lax.axis_size("core")
    full_width = channels * members
    place = lax.axis_index(LINE).astype(jnp.int32).reshape(1)
    gain = norm_gain.reshape(1, channels)
    unit = 2 * rows * DH * DH * heads
    chunks = ((plane, channels // plane, DH), LOW)
    whole = ((rows, channels), WIDE)
    result = ((rows, channels), LOW)
    buffer = pltpu.VMEM(*result)
    tiles = pltpu.VMEM((heads, 3 * half, half), LOW)
    sems = pltpu.SemaphoreType.DMA((2, rows // DH))

    (own,) = call(
        own_state_kernel, [chunks], place, key_vectors, values, flops=unit, places="shh",
        scratch=[buffer, buffer, pltpu.VMEM((heads, DH, DH), WIDE), sems], mib=53.6,
    )
    low, _ = scan_states(own, place, False)
    prefix_low = exchange(low, PLANE, PLANE_ORDER)
    attended, sums = call(
        attend_kernel,
        [whole, ((members, 2 * rows // DH, DH), WIDE)],
        queries, key_vectors, values, prefix_low, cotangent, gain, flops=7 * unit,
    )
    sums = exchange(sums, HEAD, HEAD_ORDER)
    grad, own_grad, inverse = call(
        functools.partial(grad_kernel, full_width),
        [result, chunks, ((rows // DH, DH), WIDE)],
        sums, attended, cotangent, gain, queries, flops=unit,
    )

    def products(after):
        return call(
            products_kernel,
            [result, result, whole, whole],
            grad, queries, key_vectors, values, prefix_low, attended, inverse, gain, after,
            flops=16 * unit, places="vvvvvvvva", scratch=[tiles, tiles], mib=10,
        )

    low, extra = scan_states(own_grad, place, True, products)
    query_grad, normed_out, key_part, value_part = extra
    later_low = exchange(low, PLANE, PLANE_ORDER)
    key_grad, value_grad = call(
        final_kernel,
        [result, result],
        key_vectors, values, later_low, key_part, value_part, flops=2 * unit,
        out_places="hh", scratch=[buffer, buffer, sems],
    )
    return (normed_out, query_grad, key_grad, value_grad)


def solution(mesh):
    fine = Mesh(
        mesh.devices.reshape(8, 4, 2, 4, 2), ("z_lo", "x", "core", "y", "z_hi")
    )
    placed = (P(CTX, HEAD), P(CTX, HEAD), P(CTX, HEAD), P(HEAD), P(CTX, HEAD))
    return jax.shard_map(
        on_device,
        mesh=fine,
        in_specs=placed,
        out_specs=(P(CTX, HEAD),) * 4,
        check_vma=False,
    )
```

```python
import functools

import jax
import jax.numpy as jnp
from jax import lax
from jax.experimental import pallas as pl
from jax.experimental.pallas import tpu as pltpu
from jax.sharding import Mesh, PartitionSpec as P

DH = 128
EPSILON = 1e-05
PLANE = ("x", "core")
LINE = "z_lo"
CTX = ("z_lo", "x", "core")
HEAD = ("y", "z_hi")
LINE_ORDER = [4, 5, 6, 7, 0, 1, 2, 3]
PLANE_ORDER = [5, 7, 1, 3, 2, 0, 6, 4]
HEAD_ORDER = [5, 7, 1, 3, 4, 6, 0, 2]
LOW = jnp.bfloat16
WIDE = jnp.float32


def dot(left, right, left_dim, right_dim):
    return lax.dot_general(
        left, right, (((left_dim,), (right_dim,)), ((), ())), preferred_element_type=WIDE
    )


def head_columns(head):
    return slice(head * DH, (head + 1) * DH)


def state_of(low_ref, head):
    rows = low_ref.shape[1]
    per_head = DH // rows
    return low_ref[head * per_head : (head + 1) * per_head].reshape(DH, DH)


def put_state(out_ref, head, state):
    rows = out_ref.shape[1]
    per_head = DH // rows
    out_ref[head * per_head : (head + 1) * per_head] = state.astype(LOW).reshape(
        per_head, rows, DH
    )


def causal_tile(size):
    return lax.broadcasted_iota(jnp.int32, (size, size), 0) >= lax.broadcasted_iota(
        jnp.int32, (size, size), 1
    )


def own_state_kernel(place_ref, left_hbm, right_hbm, out_ref, left_ref, right_ref, total_ref, sems):
    rows, channels = left_ref.shape
    copies = []
    for block in range(rows // DH):
        at = pl.ds(block * DH, DH)
        for side, (source, target) in enumerate(((left_hbm, left_ref), (right_hbm, right_ref))):
            copies.append(pltpu.make_async_copy(source.at[at], target.at[at], sems.at[side, block]))
            copies[-1].start()
    blocks = rows // DH
    for block in range(blocks):
        for copy in copies[2 * block : 2 * block + 2]:
            copy.wait()
        at_rows = slice(block * DH, (block + 1) * DH)
        for head in range(channels // DH):
            at = head_columns(head)
            state = dot(left_ref[at_rows, at], right_ref[at_rows, at], 0, 0)
            if block > 0:
                state = total_ref[head] + state
            if block < blocks - 1:
                total_ref[head] = state
            else:
                put_state(out_ref, head, state)


def masked_tiles(left_ref, right_ref, at, out_ref, head):
    half = left_ref.shape[0] // 2
    causal = causal_tile(half)
    first = dot(left_ref[:, at], right_ref[:half, at], 1, 1)
    last = dot(left_ref[half:, at], right_ref[half:, at], 1, 1)
    out_ref[head, :half] = jnp.where(causal, first[:half], 0.0).astype(LOW)
    out_ref[head, half : 2 * half] = first[half:].astype(LOW)
    out_ref[head, 2 * half :] = jnp.where(causal, last, 0.0).astype(LOW)


def rows_product(tiles_ref, head, right_ref, at):
    half = tiles_ref.shape[2]
    both = dot(tiles_ref[head, : 2 * half], right_ref[:half, at], 1, 0)
    last = dot(tiles_ref[head, 2 * half :], right_ref[half:, at], 1, 0)
    return both[:half], both[half:] + last


def columns_product(tiles_ref, head, right_ref, at):
    half = tiles_ref.shape[2]
    first = dot(tiles_ref[head, : 2 * half], right_ref[:, at], 0, 0)
    last = dot(tiles_ref[head, 2 * half :], right_ref[half:, at], 0, 0)
    return first, last


def totals_kernel(mine_ref, out_ref):
    total = mine_ref[0].astype(WIDE)
    for member in range(1, mine_ref.shape[0]):
        total = total + mine_ref[member].astype(WIDE)
    out_ref[...] = jnp.broadcast_to(total.astype(LOW)[None], out_ref.shape)


def chunks_kernel(backward, place_ref, mine_ref, totals_ref, *rest):
    out_ref = rest[-1]
    place = place_ref[0]
    running = jnp.zeros(mine_ref.shape[1:], WIDE)
    for slot, plane in enumerate(LINE_ORDER):
        keep = plane > place if backward else plane < place
        running = running + jnp.where(keep, totals_ref[slot].astype(WIDE), 0.0)
    members = mine_ref.shape[0]
    for member in range(members - 1, -1, -1) if backward else range(members):
        slot = PLANE_ORDER.index(member)
        out_ref[slot] = running.astype(LOW)
        running = running + mine_ref[slot].astype(WIDE)


def attend_kernel(
    query_ref, key_ref, value_ref, low_ref, cotangent_ref, gain_ref, attended_ref, sums_ref
):
    rows, channels = query_ref.shape
    half = rows // 2
    causal = causal_tile(half)
    squares = [0.0, 0.0]
    slopes = [0.0, 0.0]
    for head in range(channels // DH):
        at = head_columns(head)
        first = dot(query_ref[:, at], key_ref[:half, at], 1, 1)
        last = dot(query_ref[half:, at], key_ref[half:, at], 1, 1)
        left = jnp.concatenate([jnp.where(causal, first[:half], 0.0), first[half:]]).astype(LOW)
        left = dot(left, value_ref[:half, at], 1, 0)
        last = jnp.where(causal, last, 0.0).astype(LOW)
        intra = left[:half], left[half:] + dot(last, value_ref[half:, at], 1, 0)
        inter = dot(query_ref[:, at], state_of(low_ref, head), 1, 0)
        for part in range(2):
            at_rows = slice(part * half, (part + 1) * half)
            attended = intra[part] + inter[at_rows]
            attended_ref[at_rows, at] = attended
            squares[part] = squares[part] + attended * attended
            scaled = cotangent_ref[at_rows, at].astype(WIDE) * gain_ref[:, at]
            slopes[part] = slopes[part] + scaled * attended
    parts = []
    for sums in squares + slopes:
        for block in range(half // DH):
            turned = jnp.transpose(sums[block * DH : (block + 1) * DH])
            parts.append(jnp.sum(turned, axis=0, keepdims=True))
    packed = jnp.concatenate(parts, axis=0)
    sums_ref[...] = jnp.broadcast_to(packed[None], sums_ref.shape)


def grad_kernel(
    full_width, sums_ref, attended_ref, cotangent_ref, gain_ref, query_ref,
    grad_ref, own_ref, inverse_ref,
):
    rows, channels = query_ref.shape
    blocks = rows // DH
    total = sums_ref[0]
    for member in range(1, sums_ref.shape[0]):
        total = total + sums_ref[member]
    mean = total * (1.0 / full_width)
    inverse = lax.rsqrt(mean[:blocks] + EPSILON)
    factor = inverse * inverse * inverse * mean[blocks:]
    for block in range(blocks):
        at_rows = slice(block * DH, (block + 1) * DH)
        wide = jnp.transpose(jnp.broadcast_to(inverse[block : block + 1], (DH, DH)))
        second = jnp.transpose(jnp.broadcast_to(factor[block : block + 1], (DH, DH)))
        inverse_ref[at_rows] = wide
        for head in range(channels // DH):
            at = head_columns(head)
            scaled = cotangent_ref[at_rows, at].astype(WIDE) * gain_ref[:, at]
            grad_ref[at_rows, at] = (
                wide * scaled - second * attended_ref[at_rows, at]
            ).astype(LOW)
    for head in range(channels // DH):
        at = head_columns(head)
        put_state(own_ref, head, dot(query_ref[:, at], grad_ref[:, at], 0, 0))


def products_kernel(
    grad_ref, query_ref, key_ref, value_ref, low_ref, attended_ref, inverse_ref, gain_ref, after_ref,
    query_grad_ref, normed_ref, key_part_ref, value_part_ref, tiles_ref, grad_tiles_ref,
):
    half = grad_ref.shape[0] // 2
    inverse = inverse_ref[...]
    for head in range(grad_ref.shape[1] // DH):
        at = head_columns(head)
        masked_tiles(query_ref, key_ref, at, tiles_ref, head)
        masked_tiles(grad_ref, value_ref, at, grad_tiles_ref, head)
        inter = dot(grad_ref[:, at], state_of(low_ref, head), 1, 1)
        top, bottom = rows_product(grad_tiles_ref, head, key_ref, at)
        query_grad_ref[:half, at] = (top + inter[:half]).astype(LOW)
        query_grad_ref[half:, at] = (bottom + inter[half:]).astype(LOW)
        normed_ref[:, at] = (gain_ref[:, at] * attended_ref[:, at] * inverse).astype(LOW)
        first, last = columns_product(grad_tiles_ref, head, query_ref, at)
        key_part_ref[:half, at] = first
        key_part_ref[half:, at] = last
        first, last = columns_product(tiles_ref, head, grad_ref, at)
        value_part_ref[:half, at] = first
        value_part_ref[half:, at] = last


def final_kernel(
    key_ref, value_ref, later_ref, key_part_ref, value_part_ref, key_grad_hbm, value_grad_hbm,
    key_grad_ref, value_grad_ref, sems,
):
    rows, channels = key_ref.shape
    copies = []
    step = rows // 2
    for block in range(2):
        at_rows = slice(block * step, (block + 1) * step)
        for head in range(channels // DH):
            at = head_columns(head)
            later = state_of(later_ref, head)
            key_grad_ref[at_rows, at] = (
                key_part_ref[at_rows, at] + dot(value_ref[at_rows, at], later, 1, 1)
            ).astype(LOW)
            value_grad_ref[at_rows, at] = (
                value_part_ref[at_rows, at] + dot(key_ref[at_rows, at], later, 1, 0)
            ).astype(LOW)
        span = pl.ds(block * step, step)
        for side, (source, target) in enumerate(
            ((key_grad_ref, key_grad_hbm), (value_grad_ref, value_grad_hbm))
        ):
            copies.append(pltpu.make_async_copy(source.at[span], target.at[span], sems.at[side, block]))
            copies[-1].start()
    for copy in copies:
        copy.wait()


IN_VMEM = pl.BlockSpec(memory_space=pltpu.VMEM)
IN_SMEM = pl.BlockSpec(memory_space=pltpu.SMEM)
ANYWHERE = pl.BlockSpec(memory_space=pl.ANY)
IN_HBM = pl.BlockSpec(memory_space=pltpu.HBM)


def call(kernel, shapes, *operands, flops=0, places="", out_places="", scratch=(), mib=8):
    kinds = {"v": IN_VMEM, "s": IN_SMEM, "a": ANYWHERE, "h": IN_HBM}
    outs = tuple(jax.ShapeDtypeStruct(shape, kind) for shape, kind in shapes)
    moved = sum(a.size * a.dtype.itemsize for a in operands) + sum(
        o.size * o.dtype.itemsize for o in outs
    )
    return pl.pallas_call(
        kernel,
        out_shape=outs,
        in_specs=[kinds[k] for k in places or "v" * len(operands)],
        out_specs=tuple(kinds[k] for k in out_places or "v" * len(outs)),
        scratch_shapes=scratch,
        compiler_params=pltpu.CompilerParams(vmem_limit_bytes=int(mib * 2**20)),
        cost_estimate=pl.CostEstimate(flops=flops, bytes_accessed=moved, transcendentals=0),
    )(*operands)


def exchange(blocks, axes, order):
    return lax.all_to_all(blocks, axes, 0, 0, axis_index_groups=[order])


def scan_states(chunks, place, backward, beside=None):
    shape = (chunks.shape, LOW)
    line = lax.axis_size(LINE)
    mine = exchange(chunks, PLANE, PLANE_ORDER)
    (spread,) = call(totals_kernel, [((line,) + mine.shape[1:], LOW)], mine)
    totals = exchange(spread, LINE, LINE_ORDER)
    extra = () if beside is None else tuple(beside(spread))
    order = extra[-1:]
    (low,) = call(
        functools.partial(chunks_kernel, backward), [shape], place, mine, totals, *order,
        places="svv" + "a" * len(order),
    )
    return low, extra


def on_device(queries, key_vectors, values, norm_gain, cotangent):
    rows, channels = queries.shape
    heads = channels // DH
    half = rows // 2
    members = lax.axis_size("y") * lax.axis_size("z_hi")
    plane = lax.axis_size("x") * lax.axis_size("core")
    full_width = channels * members
    place = lax.axis_index(LINE).astype(jnp.int32).reshape(1)
    gain = norm_gain.reshape(1, channels)
    unit = 2 * rows * DH * DH * heads
    chunks = ((plane, channels // plane, DH), LOW)
    whole = ((rows, channels), WIDE)
    result = ((rows, channels), LOW)
    buffer = pltpu.VMEM(*result)
    tiles = pltpu.VMEM((heads, 3 * half, half), LOW)
    sems = pltpu.SemaphoreType.DMA((2, rows // DH))

    (own,) = call(
        own_state_kernel, [chunks], place, key_vectors, values, flops=unit, places="shh",
        scratch=[buffer, buffer, pltpu.VMEM((heads, DH, DH), WIDE), sems], mib=53.6,
    )
    low, _ = scan_states(own, place, False)
    prefix_low = exchange(low, PLANE, PLANE_ORDER)
    attended, sums = call(
        attend_kernel,
        [whole, ((members, 2 * rows // DH, DH), WIDE)],
        queries, key_vectors, values, prefix_low, cotangent, gain, flops=7 * unit,
    )
    sums = exchange(sums, HEAD, HEAD_ORDER)
    grad, own_grad, inverse = call(
        functools.partial(grad_kernel, full_width),
        [result, chunks, ((rows, DH), WIDE)],
        sums, attended, cotangent, gain, queries, flops=unit,
    )

    def products(after):
        return call(
            products_kernel,
            [result, result, whole, whole],
            grad, queries, key_vectors, values, prefix_low, attended, inverse, gain, after,
            flops=16 * unit, places="vvvvvvvva", scratch=[tiles, tiles], mib=10,
        )

    low, extra = scan_states(own_grad, place, True, products)
    query_grad, normed_out, key_part, value_part = extra
    later_low = exchange(low, PLANE, PLANE_ORDER)
    key_grad, value_grad = call(
        final_kernel,
        [result, result],
        key_vectors, values, later_low, key_part, value_part, flops=2 * unit,
        out_places="hh", scratch=[buffer, buffer, sems],
    )
    return (normed_out, query_grad, key_grad, value_grad)


def solution(mesh):
    fine = Mesh(
        mesh.devices.reshape(8, 4, 2, 4, 2), ("z_lo", "x", "core", "y", "z_hi")
    )
    placed = (P(CTX, HEAD), P(CTX, HEAD), P(CTX, HEAD), P(HEAD), P(CTX, HEAD))
    return jax.shard_map(
        on_device,
        mesh=fine,
        in_specs=placed,
        out_specs=(P(CTX, HEAD),) * 4,
        check_vma=False,
    )
```
